32 devices in a mesh: group: 2 (over x), region: 8 (over z, y), sub: 2 (over core).
Axes of the slice: x: 2, y: 2, z: 4, core: 2. Of those that a mesh axis runs over, the one named last changes fastest.
Arguments:
- node_latent: bfloat16 [6144, 512], P(('group', 'region', 'sub')), parts along dimension 0, may hold values from -6 to 6
- edge_latent: bfloat16 [49152, 512], P(('group', 'region', 'sub')), parts along dimension 0, may hold values from -6 to 6
- node_cot: bfloat16 [6144, 512], P(('group', 'region', 'sub')), parts along dimension 0, may hold values from -6 to 6
- edge_cot: bfloat16 [49152, 512], P(('group', 'region', 'sub')), parts along dimension 0, may hold values from -6 to 6
- send_rows: int32 [32, 16, 8], P(('group', 'region', 'sub')), parts along dimension 0, may hold values from 0 to 191, as said below
- edge_sender: int32 [49152], P(('group', 'region', 'sub')), parts along dimension 0, may hold values from 0 to 319, as said below
- edge_receiver: int32 [49152], P(('group', 'region', 'sub')), parts along dimension 0, may hold values from 0 to 191
- edge_first: bfloat16 [1536, 512], replicated, may hold values from -0.15625 to 0.15625
- edge_second: bfloat16 [512, 512], replicated, may hold values from -0.25 to 0.25
- edge_bias: float32 [512], replicated, may hold values from -3 to 3
- edge_gain: float32 [512], replicated, may hold values from 0.5 to 1.5
- edge_shift: float32 [512], replicated, may hold values from -3 to 3
- node_first: bfloat16 [1024, 512], replicated, may hold values from -0.1875 to 0.1875
- node_second: bfloat16 [512, 512], replicated, may hold values from -0.25 to 0.25
- node_bias: float32 [512], replicated, may hold values from -3 to 3
- node_gain: float32 [512], replicated, may hold values from 0.5 to 1.5
Outputs:
- node_grad: bfloat16 [6144, 512], P(('group', 'region', 'sub')), parts along dimension 0
- edge_grad: bfloat16 [49152, 512], P(('group', 'region', 'sub')), parts along dimension 0
- edge_first_grad: float32 [3072, 512], P(('group', 'region', 'sub')), parts along dimension 0
- edge_second_grad: float32 [1024, 512], P(('group', 'region', 'sub')), parts along dimension 0
- edge_vector_grad: float32 [6, 512], P('group', ('region', 'sub')), parts along dimension 0
- node_first_grad: float32 [2048, 512], P(('group', 'region', 'sub')), parts along dimension 0
- node_second_grad: float32 [1024, 512], P(('group', 'region', 'sub')), parts along dimension 0
- node_vector_grad: float32 [4, 512], P('group', ('region', 'sub')), parts along dimension 0
The draws below stay inside these ranges and needn't reach their ends.
There are 2 independent parts, one for each index of `group`. The reference program is written for one: setup_inputs(seed, part) draws one part's arguments, and reference() takes and returns one part's arrays. A program takes and returns all parts, laid end to end along the dimension named above; an argument that names none is the same for every part. Nothing has to cross between parts.
Inputs may be any that keep to these rules, and one draw needn't show every extreme that they name: `send_rows`: own nodes of the sending device. `edge_sender`: within each device's 1536 edges the entries ascend. An entry below 192 is an own node; an entry v at or above it is slot (v - 192) % 8 of the halo that device (v - 192) // 8 sends to this device. Some slots are named by no edge.
All inputs are finite; a program needn't handle non-finite values.
Results may differ from the reference program's by a relative error of at most 0.012.
Values may be sent and summed in bfloat16 or wider, within the bound.
A program may use at most 128 MiB of HBM per device.

```python
import math
import jax
import jax.numpy as jnp
from jax import lax

LATENT = 512
NODE_DEV = 192
SLOTS = 8
EDGE_DEV = 1536
PEERS = 16
NODES = 3072
EDGES = 24576


def draw_send_rows(key, part):
    key = jax.random.fold_in(key, 3)
    return jax.random.randint(key, (PEERS, PEERS, SLOTS), 0, NODE_DEV).astype(jnp.int32)


def draw_edge_sender(key, part):
    key = jax.random.fold_in(key, 5)
    count_key, pick_key = jax.random.split(key)
    counts = jax.random.randint(count_key, (PEERS, PEERS), 0, SLOTS + 1)
    source = jnp.arange(PEERS)[:, None]
    target = jnp.arange(PEERS)[None, :]
    beside = (target == (source + 1) % PEERS) | (target == (source + PEERS - 1) % PEERS)
    counts = jnp.where(beside, SLOTS, counts)
    counts = jnp.where(source == target, 0, counts)
    drawn_rows = jax.random.randint(pick_key, (PEERS, EDGE_DEV), 0, NODE_DEV + PEERS * SLOTS)
    offsets = jnp.maximum(drawn_rows - NODE_DEV, 0)
    anchor_peer = offsets // SLOTS
    slot_place = offsets % SLOTS
    device_rows = jnp.broadcast_to(jnp.arange(PEERS)[:, None], (PEERS, EDGE_DEV))
    live_slot = (drawn_rows >= NODE_DEV) & (slot_place < counts[anchor_peer, device_rows])
    drawn_rows = jnp.where(live_slot | (drawn_rows < NODE_DEV), drawn_rows, drawn_rows % NODE_DEV)
    forced_rows = NODE_DEV + (jnp.arange(PEERS) + 1) % PEERS * SLOTS + SLOTS - 1
    drawn_rows = drawn_rows.at[:, EDGE_DEV - 1].set(forced_rows)
    return jnp.sort(drawn_rows, axis=1).reshape(-1).astype(jnp.int32)


def place_ends(drawn, rng, low, high):
    index_at = [jax.random.randint(jax.random.fold_in(rng, axis), (), 0, length) for axis, length in enumerate(drawn.shape)]
    longest = drawn.shape.index(max(drawn.shape))
    next_to = index_at[:longest] + [(index_at[longest] + 1) % drawn.shape[longest]] + index_at[longest + 1:]
    return drawn.at[tuple(index_at)].set(low).at[tuple(next_to)].set(high)


def steps_of(stream_key, dims, pieces, low, high):
    def one(dim, parts):
        heights = jax.random.uniform(jax.random.fold_in(jax.random.fold_in(stream_key, 6), dim), (parts,), jnp.float32, low / len(pieces), high / len(pieces))
        return jnp.repeat(jnp.exp(heights), dims[dim] // parts).reshape((-1,) + (1,) * (len(dims) - dim - 1))

    level = one(*pieces[0])
    for cut in pieces[1:]:
        level = level * one(*cut)
    return level


def gaussian(stream_key, shape, scale, most, shards=(), kind=jnp.bfloat16):
    loudness = steps_of(stream_key, shape, shards, -0.22, 0.18) if shards else 1.0
    values = jax.random.normal(stream_key, shape, jnp.float32) * scale * loudness
    return jnp.minimum(jnp.maximum(values, -most), most).astype(kind)


def setup_inputs(seed: int = 0, part: int = 0) -> dict:
    seeds = jax.random.split(jax.random.key(seed), 17)
    part_keys = jax.random.split(jax.random.fold_in(seeds[16], part), 17)
    node_latent = gaussian(part_keys[0], (NODES, LATENT), 1.0, 6.0, ((0, 16),))
    edge_latent = gaussian(part_keys[1], (EDGES, LATENT), 1.0, 6.0, ((0, 16),))
    node_cot = gaussian(part_keys[2], (NODES, LATENT), 1.0, 6.0, ((0, 16),))
    edge_cot = gaussian(part_keys[3], (EDGES, LATENT), 1.0, 6.0, ((0, 16),))
    send_rows = draw_send_rows(jax.random.fold_in(jax.random.fold_in(seeds[16], part), 71), part)
    edge_sender = draw_edge_sender(jax.random.fold_in(jax.random.fold_in(seeds[16], part), 71), part)
    edge_receiver = place_ends(jax.random.randint(part_keys[6], (EDGES,), 0, NODE_DEV), jax.random.fold_in(part_keys[6], 1), 0, NODE_DEV - 1).astype(jnp.int32)
    edge_first = gaussian(seeds[7], (3 * LATENT, LATENT), (3 * LATENT) ** -0.5, 0.15625)
    edge_second = gaussian(seeds[8], (LATENT, LATENT), LATENT ** -0.5, 0.25)
    edge_bias = gaussian(seeds[9], (LATENT,), 0.5, 3.0, (), jnp.float32)
    edge_gain = jnp.clip(1.0 + 0.1 * jax.random.normal(seeds[10], (LATENT,), jnp.float32), 0.5, 1.5)
    edge_shift = gaussian(seeds[11], (LATENT,), 0.5, 3.0, (), jnp.float32)
    node_first = gaussian(seeds[12], (2 * LATENT, LATENT), (2 * LATENT) ** -0.5, 0.1875)
    node_second = gaussian(seeds[13], (LATENT, LATENT), LATENT ** -0.5, 0.25)
    node_bias = gaussian(seeds[14], (LATENT,), 0.5, 3.0, (), jnp.float32)
    node_gain = jnp.clip(1.0 + 0.1 * jax.random.normal(seeds[15], (LATENT,), jnp.float32), 0.5, 1.5)
    return dict(node_latent=node_latent, edge_latent=edge_latent, node_cot=node_cot, edge_cot=edge_cot, send_rows=send_rows, edge_sender=edge_sender, edge_receiver=edge_receiver, edge_first=edge_first, edge_second=edge_second, edge_bias=edge_bias, edge_gain=edge_gain, edge_shift=edge_shift, node_first=node_first, node_second=node_second, node_bias=node_bias, node_gain=node_gain)


def mlp_forward(inputs, first, bias, second):
    before = jnp.dot(inputs, first, preferred_element_type=jnp.float32) + bias.astype(jnp.float32)
    active = jax.nn.silu(before).astype(jnp.bfloat16)
    output = jnp.dot(active, second, preferred_element_type=jnp.float32)
    centred = output - lax.optimization_barrier(jnp.mean(output, axis=-1, keepdims=True))
    inverse = lax.rsqrt(lax.optimization_barrier(jnp.mean(centred * centred, axis=-1, keepdims=True)) + 1e-05)
    return (before, active, centred * inverse, inverse)

def mlp_backward(inputs, first, second, gain, before, active, normed, inverse, upstream):
    grad_norm = upstream * gain.astype(jnp.float32)
    centred = grad_norm - lax.optimization_barrier(jnp.mean(grad_norm, axis=-1, keepdims=True))
    grad_out = (inverse * (centred - normed * lax.optimization_barrier(jnp.mean(grad_norm * normed, axis=-1, keepdims=True)))).astype(jnp.bfloat16)
    sigmoid = jax.nn.sigmoid(before)
    grad_before = jnp.dot(grad_out, second.T, preferred_element_type=jnp.float32) * (sigmoid + before * sigmoid * (1.0 - sigmoid))
    grad_pre = grad_before.astype(jnp.bfloat16)
    grad_inputs = jnp.dot(grad_pre, first.T, preferred_element_type=jnp.float32)
    grad_first = jnp.dot(inputs.T, grad_pre, preferred_element_type=jnp.float32)
    grad_second = jnp.dot(active.T, grad_out, preferred_element_type=jnp.float32)
    return (grad_inputs, grad_first, grad_second, lax.optimization_barrier(jnp.sum(grad_before, axis=0)), lax.optimization_barrier(jnp.sum(upstream * normed, axis=0)))

def reference(node_latent, edge_latent, node_cot, edge_cot, send_rows, edge_sender, edge_receiver, edge_first, edge_second, edge_bias, edge_gain, edge_shift, node_first, node_second, node_bias, node_gain):
    owner_device = (jnp.arange(EDGES, dtype=jnp.int32) // EDGE_DEV).astype(jnp.int32)
    offsets = jnp.maximum(edge_sender - NODE_DEV, 0).astype(jnp.int32)
    anchor_peer = (offsets // SLOTS).astype(jnp.int32)
    slot_place = (offsets % SLOTS).astype(jnp.int32)
    remote_node = send_rows[anchor_peer, owner_device, slot_place]
    sender_node = jnp.where(edge_sender < NODE_DEV, owner_device * NODE_DEV + edge_sender, anchor_peer * NODE_DEV + remote_node).astype(jnp.int32)
    receiver_node = (owner_device * NODE_DEV + edge_receiver).astype(jnp.int32)
    edge_input = jnp.concatenate([edge_latent, node_latent[sender_node], node_latent[receiver_node]], axis=1)
    e_before, e_active, e_normed, e_inverse = mlp_forward(edge_input, edge_first, edge_bias, edge_second)
    message = (e_normed * edge_gain + edge_shift).astype(jnp.bfloat16)
    aggregate = jax.ops.segment_sum(message.astype(jnp.float32), receiver_node, num_segments=NODES).astype(jnp.bfloat16)
    node_input = jnp.concatenate([node_latent, aggregate], axis=1)
    n_before, n_active, n_normed, n_inverse = mlp_forward(node_input, node_first, node_bias, node_second)
    node_upstream = node_cot.astype(jnp.float32)
    n_input_grad, n_first_grad, n_second_grad, n_bias_grad, n_gain_grad = mlp_backward(node_input, node_first, node_second, node_gain, n_before, n_active, n_normed, n_inverse, node_upstream)
    message_grad = edge_cot.astype(jnp.float32) + n_input_grad[:, LATENT:][receiver_node]
    e_input_grad, e_first_grad, e_second_grad, e_bias_grad, e_gain_grad = mlp_backward(edge_input, edge_first, edge_second, edge_gain, e_before, e_active, e_normed, e_inverse, message_grad)
    edge_grad = (edge_cot.astype(jnp.float32) + e_input_grad[:, :LATENT]).astype(jnp.bfloat16)
    node_total = node_upstream + n_input_grad[:, :LATENT]
    node_total = node_total + jax.ops.segment_sum(e_input_grad[:, LATENT:2 * LATENT], sender_node, num_segments=NODES)
    node_total = node_total + jax.ops.segment_sum(e_input_grad[:, 2 * LATENT:], receiver_node, num_segments=NODES)
    edge_scale = 1.0 / math.sqrt(EDGES)
    node_scale = 1.0 / math.sqrt(NODES)
    edge_vector_grad = jnp.stack([e_bias_grad, e_gain_grad, lax.optimization_barrier(jnp.sum(message_grad, axis=0))]) * edge_scale
    node_vector_grad = jnp.stack([n_bias_grad, n_gain_grad]) * node_scale
    return (node_total.astype(jnp.bfloat16), edge_grad, e_first_grad * edge_scale, e_second_grad * edge_scale, edge_vector_grad, n_first_grad * node_scale, n_second_grad * node_scale, node_vector_grad)
```

```python
import functools
import math

import jax
import jax.numpy as jnp
from jax import lax
from jax.experimental import pallas as pl
from jax.experimental.pallas import tpu as pltpu
from jax.sharding import PartitionSpec as P

MESH = pl.DeviceIdType.MESH
F32 = jnp.float32
BF16 = jnp.bfloat16
VMEM_LIMIT = 56 * 1024 * 1024


def mm(a, b):
    return jnp.dot(a, b, preferred_element_type=F32)


def mm_nt(a, b):
    return lax.dot_general(a, b, (((1,), (1,)), ((), ())), preferred_element_type=F32)


def mm_tn(a, b):
    return lax.dot_general(a, b, (((0,), (0,)), ((), ())), preferred_element_type=F32)


def one_hot(mask):
    return jnp.where(mask, 1.0, 0.0).astype(BF16)


def fold(x, k):
    if k == 1:
        return x
    w = x.shape[-1] // k
    return jnp.concatenate([x[..., j * w : (j + 1) * w] for j in range(k)], axis=-2)


def unfold(x, k):
    if k == 1:
        return x
    m = x.shape[-2] // k
    return jnp.concatenate([x[..., j * m : (j + 1) * m, :] for j in range(k)], axis=-1)


def place(index, subs):
    return {"region": index // subs, "sub": lax.rem(index, subs)}


def greet_all(me, peers, subs):
    barrier = pltpu.get_barrier_semaphore()

    @pl.loop(1, peers)
    def _(d):
        pl.semaphore_signal(
            barrier, inc=1, device_id=place(lax.rem(me + d, peers), subs), device_id_type=MESH
        )

    return barrier


def halo_kernel(regions, subs, rows_ref, latent_ref, halo_ref, sent, got, send_sem, recv_sem):
    peers = regions * subs
    me = lax.axis_index("region") * subs + lax.axis_index("sub")
    barrier = greet_all(me, peers, subs)
    slots = halo_ref.shape[0] // peers
    nodes, latent = latent_ref.shape
    picked = mm(
        one_hot(lax.broadcasted_iota(jnp.int32, (peers * slots, nodes), 1) == rows_ref[...]),
        latent_ref[...],
    )
    packed = fold(picked.reshape(peers, slots, latent), 2).astype(BF16)
    sent[...] = packed
    pl.semaphore_wait(barrier, peers - 1)

    def copy(d, target, slot):
        return pltpu.make_async_remote_copy(
            src_ref=sent.at[target],
            dst_ref=got.at[slot],
            send_sem=send_sem.at[d],
            recv_sem=recv_sem.at[d],
            device_id=place(target, subs),
            device_id_type=MESH,
        )

    @pl.loop(1, peers)
    def _(d):
        copy(d, lax.rem(me + d, peers), me).start()

    got[me] = sent[me]

    @pl.loop(1, peers)
    def _(d):
        copy(d, lax.rem(me + d, peers), lax.rem(me + peers - d, peers)).wait_recv()

    halo_ref[...] = (
        unfold(got[...].astype(F32), 2).reshape(peers * slots, latent).astype(BF16)
    )

    @pl.loop(1, peers)
    def _(d):
        copy(d, lax.rem(me + d, peers), me).wait_send()


def layer_norm(out):
    centred = out - jnp.mean(out, axis=-1, keepdims=True)
    inverse = lax.rsqrt(jnp.mean(centred * centred, axis=-1, keepdims=True) + 1e-05)
    return centred * inverse, inverse


def norm_backward(upstream, gain, normed, inverse):
    grad_norm = upstream * gain
    centred = grad_norm - jnp.mean(grad_norm, axis=-1, keepdims=True)
    share = jnp.mean(grad_norm * normed, axis=-1, keepdims=True)
    return (inverse * (centred - normed * share)).astype(BF16)


def activate(before):
    s = jax.nn.sigmoid(before)
    return (before * s).astype(BF16), s + before * s * (1.0 - s)


def compute_kernel(
    peers,
    tile,
    nl_ref,
    el_ref,
    nc_ref,
    ec_ref,
    halo_ref,
    cols_ref,
    rows_ref,
    ef_ref,
    es_ref,
    eb_ref,
    eg_ref,
    esh_ref,
    nf_ref,
    ns_ref,
    nb_ref,
    ng_ref,
    edge_out,
    node_part,
    ret_ref,
    gef_ref,
    ges_ref,
    gnf_ref,
    gns_ref,
    hot,
    hot_t,
    table,
    projected,
    active_s,
    dsilu_s,
    normed_s,
    inverse_s,
    agg,
    sums,
    vec,
):
    edges, latent = el_ref.shape
    nodes = nl_ref.shape[0]
    halo = halo_ref.shape[0]
    total = 2 * nodes + halo
    edge_scale = 1.0 / math.sqrt(edges * peers)
    node_scale = 1.0 / math.sqrt(nodes * peers)
    steps = edges // tile
    first = ef_ref.at[pl.ds(0, latent)]
    sender = ef_ref.at[pl.ds(latent, latent)]
    receiver = ef_ref.at[pl.ds(2 * latent, latent)]

    nl = nl_ref[...]
    table[pl.ds(0, nodes), :] = nl
    table[pl.ds(nodes, halo), :] = halo_ref[...]
    projected[pl.ds(0, nodes), :] = mm(nl, receiver[...]).astype(BF16)
    projected[pl.ds(nodes, nodes + halo), :] = mm(table[...], sender[...]).astype(BF16)
    agg[...] = jnp.zeros_like(agg)
    sums[...] = jnp.zeros_like(sums)
    vec[...] = jnp.zeros_like(vec)

    @pl.loop(0, steps)
    def _(t):
        at = pl.ds(pl.multiple_of(t * tile, tile), tile)
        iota = lax.broadcasted_iota(jnp.int32, (tile, total), 1)
        h = one_hot((cols_ref[at, 0:1] == iota) | (cols_ref[at, 1:2] == iota))
        hot[at, :] = h
        iota_t = lax.broadcasted_iota(jnp.int32, (total, tile), 0)
        hot_t[:, at] = one_hot((rows_ref[0:1, at] == iota_t) | (rows_ref[1:2, at] == iota_t))
        before = mm(el_ref[at, :], first[...]) + mm(h, projected[...]) + eb_ref[...]
        active, dsilu = activate(before)
        active_s[at, :] = active
        dsilu_s[at, :] = dsilu
        normed, inverse = layer_norm(mm(active, es_ref[...]))
        normed_s[at, :] = normed
        inverse_s[at, :] = inverse
        message = (normed * eg_ref[...] + esh_ref[...]).astype(BF16)
        agg[...] += mm(hot_t[pl.ds(0, nodes), at], message)

    aggregate = agg[...].astype(BF16)
    top = nf_ref.at[pl.ds(0, latent)]
    low = nf_ref.at[pl.ds(latent, latent)]
    before = mm(nl, top[...]) + mm(aggregate, low[...]) + nb_ref[...]
    active, dsilu = activate(before)
    normed, inverse = layer_norm(mm(active, ns_ref[...]))
    cot = nc_ref[...].astype(F32)
    grad_out = norm_backward(cot, ng_ref[...], normed, inverse)
    grad_before = mm_nt(grad_out, ns_ref[...]) * dsilu
    grad_pre = grad_before.astype(BF16)
    gns_ref[...] = mm_tn(active, grad_out) * node_scale
    gnf_ref[pl.ds(0, latent), :] = mm_tn(nl, grad_pre) * node_scale
    gnf_ref[pl.ds(latent, latent), :] = mm_tn(aggregate, grad_pre) * node_scale
    node_part[...] = cot + mm_nt(grad_pre, top[...])
    spread = mm_nt(grad_pre, low[...]).astype(BF16)
    vec[3:4, :] = jnp.sum(grad_before, axis=0, keepdims=True) * node_scale
    vec[4:5, :] = jnp.sum(cot * normed, axis=0, keepdims=True) * node_scale
    agg[...] = jnp.zeros_like(agg)
    gef_ref[pl.ds(0, latent), :] = jnp.zeros((latent, latent), F32)
    ges_ref[...] = jnp.zeros_like(ges_ref)
    projected[pl.ds(0, nodes), :] = spread

    @pl.loop(0, steps)
    def _(t):
        at = pl.ds(pl.multiple_of(t * tile, tile), tile)
        cot = ec_ref[at, :].astype(F32)
        grad = cot + mm(hot[at, pl.ds(0, nodes)], projected[pl.ds(0, nodes), :])
        normed = normed_s[at, :]
        grad_out = norm_backward(grad, eg_ref[...], normed, inverse_s[at, :])
        grad_before = mm_nt(grad_out, es_ref[...]) * dsilu_s[at, :]
        grad_pre = grad_before.astype(BF16)
        vec[0:1, :] += jnp.sum(grad_before, axis=0, keepdims=True) * edge_scale
        vec[1:2, :] += jnp.sum(grad * normed, axis=0, keepdims=True) * edge_scale
        vec[2:3, :] += jnp.sum(grad, axis=0, keepdims=True) * edge_scale
        edge_out[at, :] = (cot + mm_nt(grad_pre, first[...])).astype(BF16)
        sums[...] += mm(hot_t[:, at], grad_pre)
        ges_ref[...] += mm_tn(active_s[at, :], grad_out) * edge_scale
        gef_ref[pl.ds(0, latent), :] += mm_tn(el_ref[at, :], grad_pre) * edge_scale

    received = sums[pl.ds(0, nodes), :].astype(BF16)
    sent = sums[pl.ds(nodes, nodes + halo), :].astype(BF16)
    gef_ref[pl.ds(latent, latent), :] = mm_tn(table[...], sent) * edge_scale
    gef_ref[pl.ds(2 * latent, latent), :] = mm_tn(nl, received) * edge_scale
    back = mm_nt(sent, sender[...])
    node_part[...] += back[:nodes] + mm_nt(received, receiver[...])
    slots = halo // peers
    pieces = jnp.concatenate(
        [
            back[nodes:].reshape(peers, slots, latent),
            jnp.broadcast_to(vec[...][None], (peers, 8, latent)),
        ],
        axis=1,
    )
    ret_ref[...] = pieces.astype(BF16)


def reduce_kernel(regions, subs, k, count, *refs):
    grads = refs[:count]
    ret_ref, part_ref, slots_ref = refs[count : count + 3]
    refs = refs[count + 3 :]
    node_out, vec_out = refs[:2]
    outs = refs[2 : 2 + count]
    refs = refs[2 + count :]
    got = refs[0]
    bufs = [refs[1 + 6 * c : 7 + 6 * c] for c in range(count)]
    ret_send, ret_recv, near_send, near_recv, far_send, far_recv = refs[1 + 6 * count :]

    peers = regions * subs
    outer = regions // 2
    region = lax.axis_index("region")
    sub = lax.axis_index("sub")
    me = region * subs + sub
    inner = lax.rem(region, 2)
    place_o = region // 2
    barrier = greet_all(me, peers, subs)

    def own(c, q, s):
        m = outs[c].shape[0]
        row = pl.multiple_of((q * subs + s) * m, 8)
        return fold(grads[c][pl.ds(row, m), :], k)

    for c in range(count):
        a1 = bufs[c][0]

        @pl.loop(0, regions)
        def _(q, c=c, a1=a1):
            a1[q] = own(c, q, 1 - sub).astype(BF16)

    pl.semaphore_wait(barrier, peers - 1)

    def near(c, stage, src, dst, target):
        return pltpu.make_async_remote_copy(
            src_ref=src,
            dst_ref=dst,
            send_sem=near_send.at[c, stage],
            recv_sem=near_recv.at[c, stage],
            device_id=target,
            device_id_type=MESH,
        )

    def stage_1(c):
        return near(c, 0, bufs[c][0], bufs[c][1], {"region": region, "sub": 1 - sub})

    def stage_2(c):
        other = region + 1 - 2 * inner
        return near(c, 1, bufs[c][2], bufs[c][3], {"region": other, "sub": sub})

    def stage_3(c, d, target, slot):
        return pltpu.make_async_remote_copy(
            src_ref=bufs[c][4].at[target],
            dst_ref=bufs[c][5].at[slot],
            send_sem=far_send.at[c, d],
            recv_sem=far_recv.at[c, d],
            device_id={"region": target * 2 + inner, "sub": sub},
            device_id_type=MESH,
        )

    def back(d, target, slot):
        return pltpu.make_async_remote_copy(
            src_ref=ret_ref.at[target],
            dst_ref=got.at[slot],
            send_sem=ret_send.at[d],
            recv_sem=ret_recv.at[d],
            device_id=place(target, subs),
            device_id_type=MESH,
        )

    for c in range(count):
        stage_1(c).start()

    @pl.loop(1, peers)
    def _(d):
        back(d, lax.rem(me + d, peers), me).start()

    got[me] = ret_ref[me]

    for c in range(count):
        b1, a2 = bufs[c][1:3]
        stage_1(c).wait_recv()

        @pl.loop(0, outer)
        def _(o, c=c, b1=b1, a2=a2):
            q = o * 2 + 1 - inner
            a2[o] = (own(c, q, sub) + b1[q].astype(F32)).astype(BF16)

        stage_2(c).start()

    for c in range(count):
        b1, b2, a3 = bufs[c][1], bufs[c][3], bufs[c][4]
        stage_2(c).wait_recv()

        @pl.loop(0, outer)
        def _(o, c=c, b1=b1, b2=b2, a3=a3):
            q = o * 2 + inner
            a3[o] = (own(c, q, sub) + b1[q].astype(F32) + b2[o].astype(F32)).astype(BF16)

        @pl.loop(1, outer)
        def _(d, c=c):
            stage_3(c, d, lax.rem(place_o + d, outer), place_o).start()

    @pl.loop(1, peers)
    def _(d):
        back(d, lax.rem(me + d, peers), lax.rem(me + peers - d, peers)).wait_recv()

    nodes, latent = part_ref.shape
    arrived = got[...].astype(F32)
    vec_out[...] = jnp.sum(arrived[:, 8:], axis=0)
    returned = arrived[:, :8].reshape(peers * 8, latent).astype(BF16)
    spread = one_hot(
        lax.broadcasted_iota(jnp.int32, (nodes, peers * 8), 0) == slots_ref[...]
    )
    node_out[...] = (part_ref[...] + mm(spread, returned)).astype(BF16)

    for c in range(count):
        b1, b2, b3 = bufs[c][1], bufs[c][3], bufs[c][5]

        @pl.loop(1, outer)
        def _(d, c=c):
            stage_3(
                c, d, lax.rem(place_o + d, outer), lax.rem(place_o + outer - d, outer)
            ).wait_recv()

        result = own(c, region, sub) + b1[region].astype(F32) + b2[place_o].astype(F32)

        def add(d, value, b3=b3):
            return value + b3[lax.rem(place_o + d, outer)].astype(F32)

        outs[c][...] = unfold(lax.fori_loop(1, outer, add, result), k)

    for c in range(count):
        stage_1(c).wait_send()
        stage_2(c).wait_send()

        @pl.loop(1, outer)
        def _(d, c=c):
            stage_3(c, d, lax.rem(place_o + d, outer), place_o).wait_send()

    @pl.loop(1, peers)
    def _(d):
        back(d, lax.rem(me + d, peers), me).wait_send()


def in_vmem(count):
    return [pl.BlockSpec(memory_space=pltpu.VMEM)] * count


def on_device(
    regions,
    subs,
    node_latent,
    edge_latent,
    node_cot,
    edge_cot,
    send_rows,
    edge_sender,
    edge_receiver,
    edge_first,
    edge_second,
    edge_bias,
    edge_gain,
    edge_shift,
    node_first,
    node_second,
    node_bias,
    node_gain,
):
    peers = regions * subs
    nodes, latent = node_latent.shape
    edges = edge_latent.shape[0]
    slots = send_rows.shape[2]
    halo_rows = peers * slots
    total = 2 * nodes + halo_rows
    shape = jax.ShapeDtypeStruct

    halo = pl.pallas_call(
        functools.partial(halo_kernel, regions, subs),
        out_shape=shape((halo_rows, latent), BF16),
        in_specs=in_vmem(2),
        out_specs=pl.BlockSpec(memory_space=pltpu.VMEM),
        scratch_shapes=[
            pltpu.VMEM((peers, 2 * slots, latent // 2), BF16),
            pltpu.VMEM((peers, 2 * slots, latent // 2), BF16),
            pltpu.SemaphoreType.DMA((peers,)),
            pltpu.SemaphoreType.DMA((peers,)),
        ],
        compiler_params=pltpu.CompilerParams(collective_id=0, has_side_effects=True),
    )(send_rows.reshape(halo_rows, 1), node_latent)

    tile = math.gcd(edges, 512)
    ends = (edge_receiver, edge_sender + nodes)
    row = lambda x: x.reshape(1, latent)
    edge_grad, part, ret, gef, ges, gnf, gns = pl.pallas_call(
        functools.partial(compute_kernel, peers, tile),
        out_shape=(
            shape((edges, latent), BF16),
            shape((nodes, latent), F32),
            shape((peers, slots + 8, latent), BF16),
            shape(edge_first.shape, F32),
            shape(edge_second.shape, F32),
            shape(node_first.shape, F32),
            shape(node_second.shape, F32),
        ),
        in_specs=in_vmem(16),
        out_specs=tuple(in_vmem(7)),
        scratch_shapes=[
            pltpu.VMEM((edges, total), BF16),
            pltpu.VMEM((total, edges), BF16),
            pltpu.VMEM((nodes + halo_rows, latent), BF16),
            pltpu.VMEM((total, latent), BF16),
            pltpu.VMEM((edges, latent), BF16),
            pltpu.VMEM((edges, latent), F32),
            pltpu.VMEM((edges, latent), F32),
            pltpu.VMEM((edges, 1), F32),
            pltpu.VMEM((nodes, latent), F32),
            pltpu.VMEM((total, latent), F32),
            pltpu.VMEM((8, latent), F32),
        ],
        compiler_params=pltpu.CompilerParams(vmem_limit_bytes=VMEM_LIMIT),
    )(
        node_latent,
        edge_latent,
        node_cot,
        edge_cot,
        halo,
        jnp.stack(ends, axis=1),
        jnp.stack(ends, axis=0),
        edge_first,
        edge_second,
        row(edge_bias),
        row(edge_gain),
        row(edge_shift),
        node_first,
        node_second,
        row(node_bias),
        row(node_gain),
    )

    partials = (gns, gnf, ges, gef)
    shares = [g.shape[0] // peers for g in partials]
    k = 1 if all(m % 16 == 0 for m in shares) else 2
    outer = regions // 2
    scratch = [pltpu.VMEM((peers, slots + 8, latent), BF16)]
    for m in shares:
        block = (m * k, latent // k)
        for lead in (regions, regions, outer, outer, outer, outer):
            scratch.append(pltpu.VMEM((lead,) + block, BF16))
    count = len(partials)
    sem = pltpu.SemaphoreType.DMA
    scratch += [sem((peers,)), sem((peers,)), sem((count, 2)), sem((count, 2))]
    scratch += [sem((count, outer)), sem((count, outer))]
    node_grad, vectors, gns, gnf, ges, gef = pl.pallas_call(
        functools.partial(reduce_kernel, regions, subs, k, count),
        out_shape=(
            shape((nodes, latent), BF16),
            shape((8, latent), F32),
            *(shape((m, latent), F32) for m in shares),
        ),
        in_specs=in_vmem(count + 3),
        out_specs=tuple(in_vmem(count + 2)),
        scratch_shapes=scratch,
        compiler_params=pltpu.CompilerParams(
            collective_id=1, has_side_effects=True, vmem_limit_bytes=VMEM_LIMIT
        ),
    )(*partials, ret, part, send_rows.reshape(1, halo_rows))

    width = latent // peers
    start = (lax.axis_index("region") * subs + lax.axis_index("sub")) * width
    mine = lax.dynamic_slice(vectors, (0, start), (8, width))
    return node_grad, edge_grad, gef, ges, mine[0:3], gnf, gns, mine[3:5]


def solution(mesh):
    spread = P(("group", "region", "sub"), None)
    flat = P(("group", "region", "sub"))
    vector = P("group", ("region", "sub"))
    return jax.shard_map(
        functools.partial(on_device, mesh.shape["region"], mesh.shape["sub"]),
        mesh=mesh,
        in_specs=(
            spread,
            spread,
            spread,
            spread,
            P(("group", "region", "sub"), None, None),
            flat,
            flat,
        )
        + (P(),) * 9,
        out_specs=(spread, spread, spread, spread, vector, spread, spread, vector),
        check_vma=False,
    )
```

```python
import functools
import math

import jax
import jax.numpy as jnp
from jax import lax
from jax.experimental import pallas as pl
from jax.experimental.pallas import tpu as pltpu
from jax.sharding import PartitionSpec as P

MESH = pl.DeviceIdType.MESH
F32 = jnp.float32
BF16 = jnp.bfloat16
VMEM_LIMIT = 56 * 1024 * 1024


def mm(a, b):
    return jnp.dot(a, b, preferred_element_type=F32)


def mm_nt(a, b):
    return lax.dot_general(a, b, (((1,), (1,)), ((), ())), preferred_element_type=F32)


def mm_tn(a, b):
    return lax.dot_general(a, b, (((0,), (0,)), ((), ())), preferred_element_type=F32)


def one_hot(mask):
    return jnp.where(mask, 1.0, 0.0).astype(BF16)


def fold(x, k):
    if k == 1:
        return x
    w = x.shape[-1] // k
    return jnp.concatenate([x[..., j * w : (j + 1) * w] for j in range(k)], axis=-2)


def unfold(x, k):
    if k == 1:
        return x
    m = x.shape[-2] // k
    return jnp.concatenate([x[..., j * m : (j + 1) * m, :] for j in range(k)], axis=-1)


def place(index, subs):
    return {"region": index // subs, "sub": lax.rem(index, subs)}


def greet_all(me, peers, subs):
    barrier = pltpu.get_barrier_semaphore()

    @pl.loop(1, peers)
    def _(d):
        pl.semaphore_signal(
            barrier, inc=1, device_id=place(lax.rem(me + d, peers), subs), device_id_type=MESH
        )

    return barrier


def layer_norm(out):
    centred = out - jnp.mean(out, axis=-1, keepdims=True)
    inverse = lax.rsqrt(jnp.mean(centred * centred, axis=-1, keepdims=True) + 1e-05)
    return centred * inverse, inverse


def norm_backward(upstream, gain, normed, inverse):
    grad_norm = upstream * gain
    centred = grad_norm - jnp.mean(grad_norm, axis=-1, keepdims=True)
    share = jnp.mean(grad_norm * normed, axis=-1, keepdims=True)
    return (inverse * (centred - normed * share)).astype(BF16)


def activate(before):
    s = jax.nn.sigmoid(before)
    return (before * s).astype(BF16), s + before * s * (1.0 - s)


def layer_kernel(
    regions,
    subs,
    tile,
    k,
    chunks,
    nl_ref,
    el_ref,
    nc_ref,
    ec_ref,
    slots_ref,
    es_idx,
    er_idx,
    ef_ref,
    es_ref,
    eb_ref,
    eg_ref,
    esh_ref,
    nf_ref,
    ns_ref,
    nb_ref,
    ng_ref,
    edge_out,
    small_out,
    hot,
    hot_t,
    cols,
    table,
    projected,
    active_s,
    dsilu_s,
    normed_s,
    inverse_s,
    agg,
    sums,
    vec,
    node_part,
    gns_ref,
    gnf_ref,
    ges_ref,
    gef_ref,
    halo_sent,
    halo_got,
    ret_ref,
    got,
    halo_send,
    halo_recv,
    ret_send,
    ret_recv,
    near_send,
    near_recv,
    far_send,
    far_recv,
    *bufs,
):
    peers = regions * subs
    outer = regions // 2
    region = lax.axis_index("region")
    sub = lax.axis_index("sub")
    me = region * subs + sub
    inner = lax.rem(region, 2)
    place_o = region // 2

    edges, latent = el_ref.shape
    nodes = nl_ref.shape[0]
    halo = slots_ref.shape[1]
    slots = halo // peers
    total = 2 * nodes + halo
    edge_scale = 1.0 / math.sqrt(edges * peers)
    node_scale = 1.0 / math.sqrt(nodes * peers)
    steps = edges // tile
    first = ef_ref.at[pl.ds(0, latent)]
    sender = ef_ref.at[pl.ds(latent, latent)]
    receiver = ef_ref.at[pl.ds(2 * latent, latent)]
    grads = (gns_ref, gnf_ref, ges_ref, gef_ref)
    shares = [g.shape[0] // peers for g in grads]
    starts = [sum(shares[:j]) for j in range(5)]

    barrier = greet_all(me, peers, subs)
    nl = nl_ref[...]
    slot_col = jnp.transpose(jnp.broadcast_to(slots_ref[...].astype(F32), (8, halo)))[:, 0:1]
    node_iota = lax.broadcasted_iota(jnp.int32, (halo, nodes), 1).astype(F32)
    picked = mm(one_hot(node_iota == slot_col), nl)
    halo_sent[...] = fold(picked.reshape(peers, slots, latent), 2).astype(BF16)
    pl.semaphore_wait(barrier, peers - 1)

    def halo_copy(d, target, slot):
        return pltpu.make_async_remote_copy(
            src_ref=halo_sent.at[target],
            dst_ref=halo_got.at[slot],
            send_sem=halo_send.at[d],
            recv_sem=halo_recv.at[d],
            device_id=place(target, subs),
            device_id_type=MESH,
        )

    @pl.loop(1, peers)
    def _(d):
        halo_copy(d, lax.rem(me + d, peers), me).start()

    halo_got[me] = halo_sent[me]
    table[pl.ds(0, nodes), :] = nl
    projected[pl.ds(0, nodes), :] = mm(nl, receiver[...]).astype(BF16)
    agg[...] = jnp.zeros_like(agg)
    sums[...] = jnp.zeros_like(sums)
    vec[...] = jnp.zeros_like(vec)
    cols[...] = jnp.transpose(
        jnp.concatenate(
            [
                jnp.broadcast_to(er_idx[...], (4, edges)),
                jnp.broadcast_to(es_idx[...] + nodes, (4, edges)),
            ],
            axis=0,
        ).astype(F32)
    )

    @pl.loop(0, steps)
    def _(t):
        at = pl.ds(pl.multiple_of(t * tile, tile), tile)
        iota = lax.broadcasted_iota(jnp.int32, (tile, total), 1).astype(F32)
        hot[at, :] = one_hot((cols[at, 0:1] == iota) | (cols[at, 4:5] == iota))
        iota_t = lax.broadcasted_iota(jnp.int32, (total, tile), 0)
        hot_t[:, at] = one_hot((er_idx[:, at] == iota_t) | (es_idx[:, at] + nodes == iota_t))
        dsilu_s[at, :] = mm(el_ref[at, :], first[...]) + eb_ref[...]

    @pl.loop(1, peers)
    def _(d):
        halo_copy(d, lax.rem(me + d, peers), lax.rem(me + peers - d, peers)).wait_recv()

    table[pl.ds(nodes, halo), :] = (
        unfold(halo_got[...].astype(F32), 2).reshape(halo, latent).astype(BF16)
    )
    projected[pl.ds(nodes, nodes + halo), :] = mm(table[...], sender[...]).astype(BF16)

    @pl.loop(0, steps)
    def _(t):
        at = pl.ds(pl.multiple_of(t * tile, tile), tile)
        active, dsilu = activate(dsilu_s[at, :] + mm(hot[at, :], projected[...]))
        active_s[at, :] = active
        dsilu_s[at, :] = dsilu
        normed, inverse = layer_norm(mm(active, es_ref[...]))
        normed_s[at, :] = normed
        inverse_s[at, :] = inverse
        message = (normed * eg_ref[...] + esh_ref[...]).astype(BF16)
        agg[...] += mm(hot_t[pl.ds(0, nodes), at], message)

    def own(c, q, s):
        g, col, width = chunks[c]
        m = shares[g]
        row = pl.multiple_of((q * subs + s) * m, 8)
        return fold(grads[g][pl.ds(row, m), pl.ds(col, width)], k)

    def near(c, stage, src, dst, target):
        return pltpu.make_async_remote_copy(
            src_ref=src,
            dst_ref=dst,
            send_sem=near_send.at[c, stage],
            recv_sem=near_recv.at[c, stage],
            device_id=target,
            device_id_type=MESH,
        )

    def of(c):
        return bufs[6 * c : 6 * c + 6]

    def copy_1(c):
        return near(c, 0, of(c)[0], of(c)[1], {"region": region, "sub": 1 - sub})

    def copy_2(c):
        other = region + 1 - 2 * inner
        return near(c, 1, of(c)[2], of(c)[3], {"region": other, "sub": sub})

    def copy_3(c, d, target, slot):
        return pltpu.make_async_remote_copy(
            src_ref=of(c)[4].at[target],
            dst_ref=of(c)[5].at[slot],
            send_sem=far_send.at[c, d],
            recv_sem=far_recv.at[c, d],
            device_id={"region": target * 2 + inner, "sub": sub},
            device_id_type=MESH,
        )

    def ret_copy(d, target, slot):
        return pltpu.make_async_remote_copy(
            src_ref=ret_ref.at[target],
            dst_ref=got.at[slot],
            send_sem=ret_send.at[d],
            recv_sem=ret_recv.at[d],
            device_id=place(target, subs),
            device_id_type=MESH,
        )

    def stage_1(c):
        a1 = of(c)[0]

        @pl.loop(0, regions)
        def _(q):
            a1[q] = own(c, q, 1 - sub).astype(BF16)

        copy_1(c).start()

    def stage_2(c):
        b1, a2 = of(c)[1:3]
        copy_1(c).wait_recv()

        @pl.loop(0, outer)
        def _(o):
            q = o * 2 + 1 - inner
            a2[o] = (own(c, q, sub) + b1[q].astype(F32)).astype(BF16)

        copy_2(c).start()

    def stage_3(c):
        b1, b2, a3 = of(c)[1], of(c)[3], of(c)[4]
        copy_2(c).wait_recv()

        @pl.loop(0, outer)
        def _(o):
            q = o * 2 + inner
            a3[o] = (own(c, q, sub) + b1[q].astype(F32) + b2[o].astype(F32)).astype(BF16)

        @pl.loop(1, outer)
        def _(d):
            copy_3(c, d, lax.rem(place_o + d, outer), place_o).start()

    def finish(c):
        b1, b2, b3 = of(c)[1], of(c)[3], of(c)[5]

        @pl.loop(1, outer)
        def _(d):
            source = lax.rem(place_o + outer - d, outer)
            copy_3(c, d, lax.rem(place_o + d, outer), source).wait_recv()

        result = own(c, region, sub) + b1[region].astype(F32) + b2[place_o].astype(F32)

        def add(d, value):
            return value + b3[lax.rem(place_o + d, outer)].astype(F32)

        g, col, width = chunks[c]
        value = unfold(lax.fori_loop(1, outer, add, result), k)
        small_out[pl.ds(starts[g], shares[g]), pl.ds(col, width)] = value

    node_chunks = [c for c, (g, _, _) in enumerate(chunks) if g < 2]
    second_chunks = [c for c, (g, _, _) in enumerate(chunks) if g == 2]
    first_chunks = [c for c, (g, _, _) in enumerate(chunks) if g == 3]

    aggregate = agg[...].astype(BF16)
    top = nf_ref.at[pl.ds(0, latent)]
    low = nf_ref.at[pl.ds(latent, latent)]
    before = mm(nl, top[...]) + mm(aggregate, low[...]) + nb_ref[...]
    active, dsilu = activate(before)
    normed, inverse = layer_norm(mm(active, ns_ref[...]))
    cot = nc_ref[...].astype(F32)
    grad_out = norm_backward(cot, ng_ref[...], normed, inverse)
    grad_before = mm_nt(grad_out, ns_ref[...]) * dsilu
    grad_pre = grad_before.astype(BF16)
    gns_ref[...] = mm_tn(active, grad_out) * node_scale
    gnf_ref[pl.ds(0, latent), :] = mm_tn(nl, grad_pre) * node_scale
    gnf_ref[pl.ds(latent, latent), :] = mm_tn(aggregate, grad_pre) * node_scale
    for c in node_chunks:
        stage_1(c)
    node_part[...] = cot + mm_nt(grad_pre, top[...])
    projected[pl.ds(0, nodes), :] = mm_nt(grad_pre, low[...]).astype(BF16)
    vec[3:4, :] = jnp.sum(grad_before, axis=0, keepdims=True) * node_scale
    vec[4:5, :] = jnp.sum(cot * normed, axis=0, keepdims=True) * node_scale
    gef_ref[pl.ds(0, latent), :] = jnp.zeros((latent, latent), F32)
    ges_ref[...] = jnp.zeros_like(ges_ref)

    @pl.loop(0, steps)
    def _(t):
        at = pl.ds(pl.multiple_of(t * tile, tile), tile)
        cot = ec_ref[at, :].astype(F32)
        grad = cot + mm(hot[at, pl.ds(0, nodes)], projected[pl.ds(0, nodes), :])
        normed = normed_s[at, :]
        grad_out = norm_backward(grad, eg_ref[...], normed, inverse_s[at, :])
        grad_before = mm_nt(grad_out, es_ref[...]) * dsilu_s[at, :]
        grad_pre = grad_before.astype(BF16)
        vec[0:1, :] += jnp.sum(grad_before, axis=0, keepdims=True) * edge_scale
        vec[1:2, :] += jnp.sum(grad * normed, axis=0, keepdims=True) * edge_scale
        vec[2:3, :] += jnp.sum(grad, axis=0, keepdims=True) * edge_scale
        edge_out[at, :] = (cot + mm_nt(grad_pre, first[...])).astype(BF16)
        sums[...] += mm(hot_t[:, at], grad_pre)
        ges_ref[...] += mm_tn(active_s[at, :], grad_out) * edge_scale
        gef_ref[pl.ds(0, latent), :] += mm_tn(el_ref[at, :], grad_pre) * edge_scale

        @pl.when(t == 0)
        def _():
            for c in node_chunks:
                stage_2(c)

        @pl.when(t == min(1, steps - 1))
        def _():
            for c in node_chunks:
                stage_3(c)

    for c in second_chunks:
        stage_1(c)
    received = sums[pl.ds(0, nodes), :].astype(BF16)
    sent = sums[pl.ds(nodes, nodes + halo), :].astype(BF16)
    gef_ref[pl.ds(latent, latent), :] = mm_tn(table[...], sent) * edge_scale
    gef_ref[pl.ds(2 * latent, latent), :] = mm_tn(nl, received) * edge_scale
    for c in first_chunks:
        stage_1(c)
    back = mm_nt(sent, sender[...])
    ret_ref[...] = jnp.concatenate(
        [
            back[nodes:].reshape(peers, slots, latent),
            jnp.broadcast_to(vec[...][None], (peers, 8, latent)),
        ],
        axis=1,
    ).astype(BF16)

    @pl.loop(1, peers)
    def _(d):
        ret_copy(d, lax.rem(me + d, peers), me).start()

    got[me] = ret_ref[me]
    for c in second_chunks + first_chunks:
        stage_2(c)
    node_part[...] += back[:nodes] + mm_nt(received, receiver[...])
    for c in node_chunks:
        finish(c)
    for c in second_chunks + first_chunks:
        stage_3(c)

    @pl.loop(1, peers)
    def _(d):
        ret_copy(d, lax.rem(me + d, peers), lax.rem(me + peers - d, peers)).wait_recv()

    arrived = got[...].astype(F32)
    vectors = jnp.sum(arrived[:, slots:], axis=0)
    width = latent // peers
    mine = jnp.zeros((8, width), F32)
    for p in range(peers):
        mine = jnp.where(me == p, vectors[:, p * width : (p + 1) * width], mine)
    small_out[pl.ds(starts[4], 8), pl.ds(0, width)] = mine
    returned = arrived[:, :slots].reshape(halo, latent).astype(BF16)
    spread = one_hot(lax.broadcasted_iota(jnp.int32, (nodes, halo), 0) == slots_ref[...])
    small_out[pl.ds(starts[4] + 8, nodes), :] = node_part[...] + mm(spread, returned)
    for c in second_chunks + first_chunks:
        finish(c)

    for c in range(len(chunks)):
        copy_1(c).wait_send()
        copy_2(c).wait_send()

        @pl.loop(1, outer)
        def _(d, c=c):
            copy_3(c, d, lax.rem(place_o + d, outer), place_o).wait_send()

    @pl.loop(1, peers)
    def _(d):
        halo_copy(d, lax.rem(me + d, peers), me).wait_send()
        ret_copy(d, lax.rem(me + d, peers), me).wait_send()


def split_kernel(small_ref, node_out, gns_out, gnf_out, ges_out, gef_out, ev_out, nv_out):
    row = 0
    for out in (gns_out, gnf_out, ges_out, gef_out):
        out[...] = small_ref[pl.ds(row, out.shape[0]), :]
        row += out.shape[0]
    width = ev_out.shape[1]
    vectors = small_ref[pl.ds(row, 8), :]
    ev_out[...] = vectors[0:3, :width]
    nv_out[...] = vectors[3:5, :width]
    node_out[...] = small_ref[pl.ds(row + 8, node_out.shape[0]), :].astype(BF16)


def in_vmem(count):
    return [pl.BlockSpec(memory_space=pltpu.VMEM)] * count


def on_device(
    regions,
    subs,
    node_latent,
    edge_latent,
    node_cot,
    edge_cot,
    send_rows,
    edge_sender,
    edge_receiver,
    edge_first,
    edge_second,
    edge_bias,
    edge_gain,
    edge_shift,
    node_first,
    node_second,
    node_bias,
    node_gain,
):
    peers = regions * subs
    nodes, latent = node_latent.shape
    edges = edge_latent.shape[0]
    slots = send_rows.shape[2]
    halo = peers * slots
    total = 2 * nodes + halo
    shape = jax.ShapeDtypeStruct
    tile = math.gcd(edges, 512)
    row = lambda x: x.reshape(1, -1)

    weights = (node_second, node_first, edge_second, edge_first)
    shares = [w.shape[0] // peers for w in weights]
    k = 1 if all(m % 16 == 0 for m in shares) else 2
    half = latent // 2
    chunks = ((0, 0, latent), (1, 0, half), (1, half, half))
    chunks += ((2, 0, latent), (3, 0, half), (3, half, half))
    outer = regions // 2
    sem = pltpu.SemaphoreType.DMA
    count = len(chunks)
    scratch = [
        pltpu.VMEM((edges, total), BF16),
        pltpu.VMEM((total, edges), BF16),
        pltpu.VMEM((edges, 8), F32),
        pltpu.VMEM((nodes + halo, latent), BF16),
        pltpu.VMEM((total, latent), BF16),
        pltpu.VMEM((edges, latent), BF16),
        pltpu.VMEM((edges, latent), F32),
        pltpu.VMEM((edges, latent), F32),
        pltpu.VMEM((edges, 1), F32),
        pltpu.VMEM((nodes, latent), F32),
        pltpu.VMEM((total, latent), F32),
        pltpu.VMEM((8, latent), F32),
        pltpu.VMEM((nodes, latent), F32),
        *(pltpu.VMEM(w.shape, F32) for w in weights),
        pltpu.VMEM((peers, 2 * slots, half), BF16),
        pltpu.VMEM((peers, 2 * slots, half), BF16),
        pltpu.VMEM((peers, slots + 8, latent), BF16),
        pltpu.VMEM((peers, slots + 8, latent), BF16),
        sem((peers,)),
        sem((peers,)),
        sem((peers,)),
        sem((peers,)),
        sem((count, 2)),
        sem((count, 2)),
        sem((count, outer)),
        sem((count, outer)),
    ]
    for g, _, width in chunks:
        for lead in (regions, regions, outer, outer, outer, outer):
            scratch.append(pltpu.VMEM((lead, shares[g] * k, width // k), BF16))
    small_rows = sum(shares) + 8 + nodes
    edge_grad, small = pl.pallas_call(
        functools.partial(layer_kernel, regions, subs, tile, k, chunks),
        out_shape=(shape((edges, latent), BF16), shape((small_rows, latent), F32)),
        in_specs=in_vmem(16),
        out_specs=tuple(in_vmem(2)),
        scratch_shapes=scratch,
        compiler_params=pltpu.CompilerParams(
            collective_id=0, has_side_effects=True, vmem_limit_bytes=VMEM_LIMIT
        ),
    )(
        node_latent,
        edge_latent,
        node_cot,
        edge_cot,
        row(send_rows),
        row(edge_sender),
        row(edge_receiver),
        edge_first,
        edge_second,
        row(edge_bias),
        row(edge_gain),
        row(edge_shift),
        node_first,
        node_second,
        row(node_bias),
        row(node_gain),
    )
    width = latent // peers
    node_grad, gns, gnf, ges, gef, ev, nv = pl.pallas_call(
        split_kernel,
        out_shape=(
            shape((nodes, latent), BF16),
            *(shape((m, latent), F32) for m in shares),
            shape((3, width), F32),
            shape((2, width), F32),
        ),
        in_specs=in_vmem(1),
        out_specs=tuple(in_vmem(7)),
    )(small)
    return node_grad, edge_grad, gef, ges, ev, gnf, gns, nv


def solution(mesh):
    spread = P(("group", "region", "sub"), None)
    flat = P(("group", "region", "sub"))
    vector = P("group", ("region", "sub"))
    return jax.shard_map(
        functools.partial(on_device, mesh.shape["region"], mesh.shape["sub"]),
        mesh=mesh,
        in_specs=(
            spread,
            spread,
            spread,
            spread,
            P(("group", "region", "sub"), None, None),
            flat,
            flat,
        )
        + (P(),) * 9,
        out_specs=(spread, spread, spread, spread, vector, spread, spread, vector),
        check_vma=False,
    )
```

```python
import functools
import math

import jax
import jax.numpy as jnp
from jax import lax
from jax.experimental import pallas as pl
from jax.experimental.pallas import tpu as pltpu
from jax.sharding import PartitionSpec as P

MESH = pl.DeviceIdType.MESH
F32 = jnp.float32
BF16 = jnp.bfloat16
VMEM_LIMIT = 56 * 1024 * 1024


def mm(a, b):
    return jnp.dot(a, b, preferred_element_type=F32)


def mm_nt(a, b):
    return lax.dot_general(a, b, (((1,), (1,)), ((), ())), preferred_element_type=F32)


def mm_tn(a, b):
    return lax.dot_general(a, b, (((0,), (0,)), ((), ())), preferred_element_type=F32)


def one_hot(mask):
    return jnp.where(mask, 1.0, 0.0).astype(BF16)


def fold(x, k):
    if k == 1:
        return x
    w = x.shape[-1] // k
    return jnp.concatenate([x[..., j * w : (j + 1) * w] for j in range(k)], axis=-2)


def unfold(x, k):
    if k == 1:
        return x
    m = x.shape[-2] // k
    return jnp.concatenate([x[..., j * m : (j + 1) * m, :] for j in range(k)], axis=-1)


def place(index, subs):
    return {"region": index // subs, "sub": lax.rem(index, subs)}


def greet_all(me, peers, subs):
    barrier = pltpu.get_barrier_semaphore()

    @pl.loop(1, peers)
    def _(d):
        pl.semaphore_signal(
            barrier, inc=1, device_id=place(lax.rem(me + d, peers), subs), device_id_type=MESH
        )

    return barrier


def layer_norm(out):
    centred = out - jnp.mean(out, axis=-1, keepdims=True)
    inverse = lax.rsqrt(jnp.mean(centred * centred, axis=-1, keepdims=True) + 1e-05)
    return centred * inverse, inverse


def norm_backward(upstream, gain, normed, inverse):
    grad_norm = upstream * gain
    centred = grad_norm - jnp.mean(grad_norm, axis=-1, keepdims=True)
    share = jnp.mean(grad_norm * normed, axis=-1, keepdims=True)
    return (inverse * (centred - normed * share)).astype(BF16)


def activate(before):
    s = jax.nn.sigmoid(before)
    return (before * s).astype(BF16), s + before * s * (1.0 - s)


def layer_kernel(
    regions,
    subs,
    tile,
    k,
    chunks,
    nl_ref,
    el_hbm,
    nc_ref,
    ec_hbm,
    send_ref,
    es_idx,
    er_idx,
    ef_hbm,
    es_hbm,
    eb_ref,
    eg_ref,
    esh_ref,
    nf_hbm,
    ns_hbm,
    nb_ref,
    ng_ref,
    edge_hbm,
    small_out,
    el_ref,
    ec_ref,
    ef_ref,
    es_ref,
    nf_ref,
    ns_ref,
    edge_out,
    grad_out_s,
    grad_pre_s,
    load_sem,
    out_sem,
    hot,
    hot_t,
    rows,
    cols,
    table,
    projected,
    active_s,
    dsilu_s,
    normed_s,
    inverse_s,
    agg,
    sums,
    vec,
    node_part,
    gns_ref,
    gnf_ref,
    ges_ref,
    gef_ref,
    halo_sent,
    halo_got,
    ret_ref,
    got,
    halo_send,
    halo_recv,
    ret_send,
    ret_recv,
    near_send,
    near_recv,
    far_send,
    far_recv,
    *bufs,
):
    peers = regions * subs
    outer = regions // 2
    region = lax.axis_index("region")
    sub = lax.axis_index("sub")
    me = region * subs + sub
    inner = lax.rem(region, 2)
    place_o = region // 2

    edges, latent = el_ref.shape
    nodes = nl_ref.shape[0]
    slots = send_ref.shape[2]
    halo = peers * slots
    total = 2 * nodes + halo
    edge_scale = 1.0 / math.sqrt(edges * peers)
    node_scale = 1.0 / math.sqrt(nodes * peers)
    steps = edges // tile
    first = ef_ref.at[pl.ds(0, latent)]
    sender = ef_ref.at[pl.ds(latent, latent)]
    receiver = ef_ref.at[pl.ds(2 * latent, latent)]
    grads = (gns_ref, gnf_ref, ges_ref, gef_ref)
    shares = [g.shape[0] // peers for g in grads]
    starts = [sum(shares[:j]) for j in range(5)]

    loads = [
        pltpu.make_async_copy(source, target, load_sem.at[j])
        for j, (source, target) in enumerate(
            (
                (ef_hbm, ef_ref),
                (el_hbm, el_ref),
                (es_hbm, es_ref),
                (nf_hbm, nf_ref),
                (ns_hbm, ns_ref),
                (ec_hbm, ec_ref),
            )
        )
    ]

    barrier = greet_all(me, peers, subs)
    for load in loads:
        load.start()
    nl = nl_ref[...]
    column = lax.broadcasted_iota(jnp.int32, (slots, halo), 1)
    repeat = jnp.where(
        lax.rem(column, slots) == lax.broadcasted_iota(jnp.int32, (slots, halo), 0), 1.0, 0.0
    )
    tiled = jnp.dot(
        send_ref[0].astype(F32),
        repeat,
        precision=lax.Precision.HIGHEST,
        preferred_element_type=F32,
    )
    column = lax.broadcasted_iota(jnp.int32, (peers, halo), 1)
    peer = lax.broadcasted_iota(jnp.int32, (peers, halo), 0) * slots
    live = (column >= peer) & (column < peer + slots)
    slot_row = jnp.round(jnp.sum(jnp.where(live, tiled, 0.0), axis=0, keepdims=True))
    slot_col = jnp.transpose(jnp.broadcast_to(slot_row, (8, halo)))[:, 0:1]
    node_iota = lax.broadcasted_iota(jnp.int32, (halo, nodes), 1).astype(F32)
    picked = mm(one_hot(node_iota == slot_col), nl)
    halo_sent[...] = fold(picked.reshape(peers, slots, latent), 2).astype(BF16)
    pl.semaphore_wait(barrier, peers - 1)

    def halo_copy(d, target, slot):
        return pltpu.make_async_remote_copy(
            src_ref=halo_sent.at[target],
            dst_ref=halo_got.at[slot],
            send_sem=halo_send.at[d],
            recv_sem=halo_recv.at[d],
            device_id=place(target, subs),
            device_id_type=MESH,
        )

    @pl.loop(1, peers)
    def _(d):
        halo_copy(d, lax.rem(me + d, peers), me).start()

    halo_got[me] = halo_sent[me]
    table[pl.ds(0, nodes), :] = nl
    agg[...] = jnp.zeros_like(agg)
    sums[...] = jnp.zeros_like(sums)
    vec[...] = jnp.zeros_like(vec)
    rows[...] = jnp.concatenate(
        [
            jnp.broadcast_to(er_idx[...][None, :], (4, edges)),
            jnp.broadcast_to(es_idx[...][None, :] + nodes, (4, edges)),
        ],
        axis=0,
    ).astype(F32)
    cols[...] = jnp.transpose(rows[...])
    loads[0].wait()
    projected[pl.ds(0, nodes), :] = mm(nl, receiver[...]).astype(BF16)
    loads[1].wait()

    @pl.loop(0, steps)
    def _(t):
        at = pl.ds(pl.multiple_of(t * tile, tile), tile)
        iota = lax.broadcasted_iota(jnp.int32, (tile, total), 1).astype(F32)
        hot[at, :] = one_hot((cols[at, 0:1] == iota) | (cols[at, 4:5] == iota))
        iota_t = lax.broadcasted_iota(jnp.int32, (total, tile), 0).astype(F32)
        hot_t[:, at] = one_hot((rows[0:1, at] == iota_t) | (rows[4:5, at] == iota_t))
        dsilu_s[at, :] = mm(el_ref[at, :], first[...]) + eb_ref[...]

    @pl.loop(1, peers)
    def _(d):
        halo_copy(d, lax.rem(me + d, peers), lax.rem(me + peers - d, peers)).wait_recv()

    table[pl.ds(nodes, halo), :] = (
        unfold(halo_got[...].astype(F32), 2).reshape(halo, latent).astype(BF16)
    )
    projected[pl.ds(nodes, nodes + halo), :] = mm(table[...], sender[...]).astype(BF16)

    loads[2].wait()

    @pl.loop(0, steps)
    def _(t):
        at = pl.ds(pl.multiple_of(t * tile, tile), tile)
        active, dsilu = activate(dsilu_s[at, :] + mm(hot[at, :], projected[...]))
        active_s[at, :] = active
        dsilu_s[at, :] = dsilu
        normed, inverse = layer_norm(mm(active, es_ref[...]))
        normed_s[at, :] = normed
        inverse_s[at, :] = inverse
        message = (normed * eg_ref[...] + esh_ref[...]).astype(BF16)
        agg[...] += mm(hot_t[pl.ds(0, nodes), at], message)

    def own(c, q, s):
        g, col, width = chunks[c]
        m = shares[g]
        row = pl.multiple_of((q * subs + s) * m, 8)
        return fold(grads[g][pl.ds(row, m), pl.ds(col, width)], k)

    def near(c, stage, src, dst, target):
        return pltpu.make_async_remote_copy(
            src_ref=src,
            dst_ref=dst,
            send_sem=near_send.at[c, stage],
            recv_sem=near_recv.at[c, stage],
            device_id=target,
            device_id_type=MESH,
        )

    def of(c):
        return bufs[6 * c : 6 * c + 6]

    def copy_1(c):
        return near(c, 0, of(c)[0], of(c)[1], {"region": region, "sub": 1 - sub})

    def copy_2(c):
        other = region + 1 - 2 * inner
        return near(c, 1, of(c)[2], of(c)[3], {"region": other, "sub": sub})

    def copy_3(c, d, target, slot):
        return pltpu.make_async_remote_copy(
            src_ref=of(c)[4].at[target],
            dst_ref=of(c)[5].at[slot],
            send_sem=far_send.at[c, d],
            recv_sem=far_recv.at[c, d],
            device_id={"region": target * 2 + inner, "sub": sub},
            device_id_type=MESH,
        )

    def ret_copy(d, target, slot):
        return pltpu.make_async_remote_copy(
            src_ref=ret_ref.at[target],
            dst_ref=got.at[slot],
            send_sem=ret_send.at[d],
            recv_sem=ret_recv.at[d],
            device_id=place(target, subs),
            device_id_type=MESH,
        )

    def stage_1(c):
        a1 = of(c)[0]

        @pl.loop(0, regions)
        def _(q):
            a1[q] = own(c, q, 1 - sub).astype(BF16)

        copy_1(c).start()

    def stage_2(c):
        b1, a2 = of(c)[1:3]
        copy_1(c).wait_recv()

        @pl.loop(0, outer)
        def _(o):
            q = o * 2 + 1 - inner
            a2[o] = (own(c, q, sub) + b1[q].astype(F32)).astype(BF16)

        copy_2(c).start()

    def stage_3(c):
        b1, b2, a3 = of(c)[1], of(c)[3], of(c)[4]
        copy_2(c).wait_recv()

        @pl.loop(0, outer)
        def _(o):
            q = o * 2 + inner
            a3[o] = (own(c, q, sub) + b1[q].astype(F32) + b2[o].astype(F32)).astype(BF16)

        @pl.loop(1, outer)
        def _(d):
            copy_3(c, d, lax.rem(place_o + d, outer), place_o).start()

    def finish(c):
        b1, b2, b3 = of(c)[1], of(c)[3], of(c)[5]

        @pl.loop(1, outer)
        def _(d):
            source = lax.rem(place_o + outer - d, outer)
            copy_3(c, d, lax.rem(place_o + d, outer), source).wait_recv()

        result = own(c, region, sub) + b1[region].astype(F32) + b2[place_o].astype(F32)

        def add(d, value):
            return value + b3[lax.rem(place_o + d, outer)].astype(F32)

        g, col, width = chunks[c]
        value = unfold(lax.fori_loop(1, outer, add, result), k)
        small_out[pl.ds(starts[g], shares[g]), pl.ds(col, width)] = value

    node_chunks = [c for c, (g, _, _) in enumerate(chunks) if g < 2]
    second_chunks = [c for c, (g, _, _) in enumerate(chunks) if g == 2]
    first_chunks = [c for c, (g, _, _) in enumerate(chunks) if g == 3]

    loads[3].wait()
    loads[4].wait()
    aggregate = agg[...].astype(BF16)
    top = nf_ref.at[pl.ds(0, latent)]
    low = nf_ref.at[pl.ds(latent, latent)]
    before = mm(nl, top[...]) + mm(aggregate, low[...]) + nb_ref[...]
    active, dsilu = activate(before)
    normed, inverse = layer_norm(mm(active, ns_ref[...]))
    cot = nc_ref[...].astype(F32)
    grad_out = norm_backward(cot, ng_ref[...], normed, inverse)
    grad_before = mm_nt(grad_out, ns_ref[...]) * dsilu
    grad_pre = grad_before.astype(BF16)
    gns_ref[...] = mm_tn(active, grad_out) * node_scale
    gnf_ref[pl.ds(0, latent), :] = mm_tn(nl, grad_pre) * node_scale
    gnf_ref[pl.ds(latent, latent), :] = mm_tn(aggregate, grad_pre) * node_scale
    for c in node_chunks:
        stage_1(c)
    node_part[...] = cot + mm_nt(grad_pre, top[...])
    projected[pl.ds(0, nodes), :] = mm_nt(grad_pre, low[...]).astype(BF16)
    vec[3:4, :] = jnp.sum(grad_before, axis=0, keepdims=True) * node_scale
    vec[4:5, :] = jnp.sum(cot * normed, axis=0, keepdims=True) * node_scale
    gef_ref[pl.ds(0, latent), :] = jnp.zeros((latent, latent), F32)
    ges_ref[...] = jnp.zeros_like(ges_ref)

    loads[5].wait()

    @pl.loop(0, steps)
    def _(t):
        at = pl.ds(pl.multiple_of(t * tile, tile), tile)
        cot = ec_ref[at, :].astype(F32)
        grad = cot + mm(hot[at, pl.ds(0, nodes)], projected[pl.ds(0, nodes), :])
        normed = normed_s[at, :]
        grad_out = norm_backward(grad, eg_ref[...], normed, inverse_s[at, :])
        grad_out_s[at, :] = grad_out
        vec[1:2, :] += jnp.sum(grad * normed, axis=0, keepdims=True) * edge_scale
        vec[2:3, :] += jnp.sum(grad, axis=0, keepdims=True) * edge_scale
        ges_ref[...] += mm_tn(active_s[at, :], grad_out) * edge_scale

    for c in second_chunks:
        stage_1(c)
    for c in node_chunks:
        stage_2(c)

    @pl.loop(0, steps)
    def _(t):
        at = pl.ds(pl.multiple_of(t * tile, tile), tile)
        grad_before = mm_nt(grad_out_s[at, :], es_ref[...]) * dsilu_s[at, :]
        grad_pre = grad_before.astype(BF16)
        grad_pre_s[at, :] = grad_pre
        vec[0:1, :] += jnp.sum(grad_before, axis=0, keepdims=True) * edge_scale
        sums[...] += mm(hot_t[:, at], grad_pre)
        gef_ref[pl.ds(0, latent), :] += mm_tn(el_ref[at, :], grad_pre) * edge_scale

        @pl.when(t == min(1, steps - 1))
        def _():
            for c in second_chunks:
                stage_2(c)
            for c in node_chunks:
                stage_3(c)

    received = sums[pl.ds(0, nodes), :].astype(BF16)
    sent = sums[pl.ds(nodes, nodes + halo), :].astype(BF16)
    gef_ref[pl.ds(latent, latent), :] = mm_tn(table[...], sent) * edge_scale
    gef_ref[pl.ds(2 * latent, latent), :] = mm_tn(nl, received) * edge_scale
    for c in first_chunks:
        stage_1(c)
    back = mm_nt(sent, sender[...])
    ret_ref[...] = jnp.concatenate(
        [
            back[nodes:].reshape(peers, slots, latent),
            jnp.broadcast_to(vec[...][None], (peers, 8, latent)),
        ],
        axis=1,
    ).astype(BF16)
    for c in first_chunks:
        stage_2(c)

    @pl.loop(1, peers)
    def _(d):
        ret_copy(d, lax.rem(me + d, peers), me).start()

    got[me] = ret_ref[me]
    for c in second_chunks:
        stage_3(c)
    node_part[...] += back[:nodes] + mm_nt(received, receiver[...])

    def edge_copy(t):
        at = pl.ds(pl.multiple_of(t * tile, tile), tile)
        return pltpu.make_async_copy(edge_out.at[at], edge_hbm.at[at], out_sem.at[t])

    @pl.loop(0, steps)
    def _(t):
        at = pl.ds(pl.multiple_of(t * tile, tile), tile)
        cot = ec_ref[at, :].astype(F32)
        edge_out[at, :] = (cot + mm_nt(grad_pre_s[at, :], first[...])).astype(BF16)
        edge_copy(t).start()

    for c in first_chunks:
        stage_3(c)
    for c in node_chunks + second_chunks:
        finish(c)

    @pl.loop(1, peers)
    def _(d):
        ret_copy(d, lax.rem(me + d, peers), lax.rem(me + peers - d, peers)).wait_recv()

    arrived = got[...].astype(F32)
    vectors = jnp.sum(arrived[:, slots:], axis=0)
    width = latent // peers
    mine = jnp.zeros((8, width), F32)
    for p in range(peers):
        mine = jnp.where(me == p, vectors[:, p * width : (p + 1) * width], mine)
    small_out[pl.ds(starts[4], 8), pl.ds(0, width)] = mine
    returned = arrived[:, :slots].reshape(halo, latent).astype(BF16)
    spread = one_hot(
        lax.broadcasted_iota(jnp.int32, (nodes, halo), 0).astype(F32) == slot_row
    )
    small_out[pl.ds(starts[4] + 8, nodes), :] = node_part[...] + mm(spread, returned)
    for c in first_chunks:
        finish(c)

    @pl.loop(0, steps)
    def _(t):
        edge_copy(t).wait()

    for c in range(len(chunks)):
        copy_1(c).wait_send()
        copy_2(c).wait_send()

        @pl.loop(1, outer)
        def _(d, c=c):
            copy_3(c, d, lax.rem(place_o + d, outer), place_o).wait_send()

    @pl.loop(1, peers)
    def _(d):
        halo_copy(d, lax.rem(me + d, peers), me).wait_send()
        ret_copy(d, lax.rem(me + d, peers), me).wait_send()


def split_kernel(
    small_ref, edge_ref, node_out, gns_out, gnf_out, ges_out, gef_out, ev_out, nv_out, edge_out, sem
):
    parts = sem.shape[0]
    each = edge_ref.shape[0] // parts
    copies = [
        pltpu.make_async_copy(
            edge_ref.at[pl.ds(j * each, each)], edge_out.at[pl.ds(j * each, each)], sem.at[j]
        )
        for j in range(parts)
    ]
    for copy in copies:
        copy.start()
    row = 0
    for out in (gns_out, gnf_out, ges_out, gef_out):
        out[...] = small_ref[pl.ds(row, out.shape[0]), :]
        row += out.shape[0]
    width = ev_out.shape[1]
    vectors = small_ref[pl.ds(row, 8), :]
    ev_out[...] = vectors[0:3, :width]
    nv_out[...] = vectors[3:5, :width]
    node_out[...] = small_ref[pl.ds(row + 8, node_out.shape[0]), :].astype(BF16)
    for copy in copies:
        copy.wait()


def in_vmem(count):
    return [pl.BlockSpec(memory_space=pltpu.VMEM)] * count


def on_device(
    regions,
    subs,
    node_latent,
    edge_latent,
    node_cot,
    edge_cot,
    send_rows,
    edge_sender,
    edge_receiver,
    edge_first,
    edge_second,
    edge_bias,
    edge_gain,
    edge_shift,
    node_first,
    node_second,
    node_bias,
    node_gain,
):
    peers = regions * subs
    nodes, latent = node_latent.shape
    edges = edge_latent.shape[0]
    slots = send_rows.shape[2]
    halo = peers * slots
    total = 2 * nodes + halo
    shape = jax.ShapeDtypeStruct
    tile = math.gcd(edges, 512)
    row = lambda x: x.reshape(1, -1)

    weights = (node_second, node_first, edge_second, edge_first)
    shares = [w.shape[0] // peers for w in weights]
    k = 1 if all(m % 16 == 0 for m in shares) else 2
    half = latent // 2
    chunks = ((0, 0, latent), (1, 0, half), (1, half, half))
    chunks += ((2, 0, latent), (3, 0, half), (3, half, half))
    outer = regions // 2
    sem = pltpu.SemaphoreType.DMA
    count = len(chunks)
    scratch = [
        pltpu.VMEM((edges, latent), BF16),
        pltpu.VMEM((edges, latent), BF16),
        pltpu.VMEM(edge_first.shape, BF16),
        pltpu.VMEM(edge_second.shape, BF16),
        pltpu.VMEM(node_first.shape, BF16),
        pltpu.VMEM(node_second.shape, BF16),
        pltpu.VMEM((edges, latent), BF16),
        pltpu.VMEM((edges, latent), BF16),
        pltpu.VMEM((edges, latent), BF16),
        sem((6,)),
        sem((edges // tile,)),
        pltpu.VMEM((edges, total), BF16),
        pltpu.VMEM((total, edges), BF16),
        pltpu.VMEM((8, edges), F32),
        pltpu.VMEM((edges, 8), F32),
        pltpu.VMEM((nodes + halo, latent), BF16),
        pltpu.VMEM((total, latent), BF16),
        pltpu.VMEM((edges, latent), BF16),
        pltpu.VMEM((edges, latent), F32),
        pltpu.VMEM((edges, latent), F32),
        pltpu.VMEM((edges, 1), F32),
        pltpu.VMEM((nodes, latent), F32),
        pltpu.VMEM((total, latent), F32),
        pltpu.VMEM((8, latent), F32),
        pltpu.VMEM((nodes, latent), F32),
        *(pltpu.VMEM(w.shape, F32) for w in weights),
        pltpu.VMEM((peers, 2 * slots, half), BF16),
        pltpu.VMEM((peers, 2 * slots, half), BF16),
        pltpu.VMEM((peers, slots + 8, latent), BF16),
        pltpu.VMEM((peers, slots + 8, latent), BF16),
        sem((peers,)),
        sem((peers,)),
        sem((peers,)),
        sem((peers,)),
        sem((count, 2)),
        sem((count, 2)),
        sem((count, outer)),
        sem((count, outer)),
    ]
    for g, _, width in chunks:
        for lead in (regions, regions, outer, outer, outer, outer):
            scratch.append(pltpu.VMEM((lead, shares[g] * k, width // k), BF16))
    in_hbm = pl.BlockSpec(memory_space=pl.ANY)
    small_rows = sum(shares) + 8 + nodes
    edge_grad, small = pl.pallas_call(
        functools.partial(layer_kernel, regions, subs, tile, k, chunks),
        out_shape=(shape((edges, latent), BF16), shape((small_rows, latent), F32)),
        in_specs=[in_hbm if j in (1, 3, 7, 8, 12, 13) else in_vmem(1)[0] for j in range(16)],
        out_specs=(in_hbm, *in_vmem(1)),
        scratch_shapes=scratch,
        compiler_params=pltpu.CompilerParams(
            collective_id=0, has_side_effects=True, vmem_limit_bytes=VMEM_LIMIT
        ),
    )(
        node_latent,
        edge_latent,
        node_cot,
        edge_cot,
        send_rows,
        edge_sender,
        edge_receiver,
        edge_first,
        edge_second,
        row(edge_bias),
        row(edge_gain),
        row(edge_shift),
        node_first,
        node_second,
        row(node_bias),
        row(node_gain),
    )
    width = latent // peers
    node_grad, gns, gnf, ges, gef, ev, nv, edge_grad = pl.pallas_call(
        split_kernel,
        out_shape=(
            shape((nodes, latent), BF16),
            *(shape((m, latent), F32) for m in shares),
            shape((3, width), F32),
            shape((2, width), F32),
            shape((edges, latent), BF16),
        ),
        in_specs=[*in_vmem(1), in_hbm],
        out_specs=(*in_vmem(7), in_hbm),
        scratch_shapes=[sem((math.gcd(edges // 16, 8),))],
        compiler_params=pltpu.CompilerParams(vmem_limit_bytes=VMEM_LIMIT),
    )(small, edge_grad)
    return node_grad, edge_grad, gef, ges, ev, gnf, gns, nv


def solution(mesh):
    spread = P(("group", "region", "sub"), None)
    flat = P(("group", "region", "sub"))
    vector = P("group", ("region", "sub"))
    return jax.shard_map(
        functools.partial(on_device, mesh.shape["region"], mesh.shape["sub"]),
        mesh=mesh,
        in_specs=(
            spread,
            spread,
            spread,
            spread,
            P(("group", "region", "sub"), None, None),
            flat,
            flat,
        )
        + (P(),) * 9,
        out_specs=(spread, spread, spread, spread, vector, spread, spread, vector),
        check_vma=False,
    )
```

```python
import functools
import math

import jax
import jax.numpy as jnp
from jax import lax
from jax.experimental import pallas as pl
from jax.experimental.pallas import tpu as pltpu
from jax.sharding import PartitionSpec as P

MESH = pl.DeviceIdType.MESH
F32 = jnp.float32
BF16 = jnp.bfloat16
VMEM_LIMIT = 56 * 1024 * 1024


def mm(a, b):
    return jnp.dot(a, b, preferred_element_type=F32)


def mm_nt(a, b):
    return lax.dot_general(a, b, (((1,), (1,)), ((), ())), preferred_element_type=F32)


def mm_tn(a, b):
    return lax.dot_general(a, b, (((0,), (0,)), ((), ())), preferred_element_type=F32)


def one_hot(mask):
    return jnp.where(mask, 1.0, 0.0).astype(BF16)


def fold(x, k):
    if k == 1:
        return x
    w = x.shape[-1] // k
    return jnp.concatenate([x[..., j * w : (j + 1) * w] for j in range(k)], axis=-2)


def unfold(x, k):
    if k == 1:
        return x
    m = x.shape[-2] // k
    return jnp.concatenate([x[..., j * m : (j + 1) * m, :] for j in range(k)], axis=-1)


def place(index, subs):
    return {"region": index // subs, "sub": lax.rem(index, subs)}


def greet_all(me, peers, subs):
    barrier = pltpu.get_barrier_semaphore()

    @pl.loop(1, peers)
    def _(d):
        pl.semaphore_signal(
            barrier, inc=1, device_id=place(lax.rem(me + d, peers), subs), device_id_type=MESH
        )

    return barrier


def layer_norm(out):
    centred = out - jnp.mean(out, axis=-1, keepdims=True)
    inverse = lax.rsqrt(jnp.mean(centred * centred, axis=-1, keepdims=True) + 1e-05)
    return centred * inverse, inverse


def norm_backward(upstream, gain, normed, inverse):
    grad_norm = upstream * gain
    centred = grad_norm - jnp.mean(grad_norm, axis=-1, keepdims=True)
    share = jnp.mean(grad_norm * normed, axis=-1, keepdims=True)
    return (inverse * (centred - normed * share)).astype(BF16)


def activate(before):
    s = jax.nn.sigmoid(before)
    return (before * s).astype(BF16), s + before * s * (1.0 - s)


def layer_kernel(
    regions,
    subs,
    tile,
    k,
    chunks,
    nl_ref,
    el_hbm,
    nc_ref,
    ec_hbm,
    send_ref,
    es_idx,
    er_idx,
    ef_hbm,
    es_hbm,
    eb_ref,
    eg_ref,
    esh_ref,
    nf_hbm,
    ns_hbm,
    nb_ref,
    ng_ref,
    edge_hbm,
    small_out,
    el_ref,
    ec_ref,
    ef_ref,
    es_ref,
    nf_ref,
    ns_ref,
    edge_out,
    grad_out_s,
    grad_pre_s,
    load_sem,
    out_sem,
    hot,
    hot_t,
    rows,
    cols,
    table,
    projected,
    active_s,
    dsilu_s,
    normed_s,
    inverse_s,
    agg,
    sums,
    vec,
    node_part,
    gns_ref,
    gnf_ref,
    ges_ref,
    gef_ref,
    halo_sent,
    halo_got,
    ret_ref,
    got,
    halo_send,
    halo_recv,
    ret_send,
    ret_recv,
    near_send,
    near_recv,
    far_send,
    far_recv,
    *bufs,
):
    peers = regions * subs
    outer = regions // 2
    region = lax.axis_index("region")
    sub = lax.axis_index("sub")
    me = region * subs + sub
    inner = lax.rem(region, 2)
    place_o = region // 2

    edges, latent = el_ref.shape
    nodes = nl_ref.shape[0]
    slots = send_ref.shape[1]
    halo = peers * slots
    total = 2 * nodes + halo
    edge_scale = 1.0 / math.sqrt(edges * peers)
    node_scale = 1.0 / math.sqrt(nodes * peers)
    steps = edges // tile
    first = ef_ref.at[pl.ds(0, latent)]
    sender = ef_ref.at[pl.ds(latent, latent)]
    receiver = ef_ref.at[pl.ds(2 * latent, latent)]
    grads = (gns_ref, gnf_ref, ges_ref, gef_ref)
    shares = [g.shape[0] // peers for g in grads]
    starts = [sum(shares[:j]) for j in range(5)]

    loads = [
        pltpu.make_async_copy(source, target, load_sem.at[j])
        for j, (source, target) in enumerate(
            (
                (ef_hbm, ef_ref),
                (el_hbm, el_ref),
                (es_hbm, es_ref),
                (nf_hbm, nf_ref),
                (ns_hbm, ns_ref),
                (ec_hbm, ec_ref),
            )
        )
    ]

    barrier = greet_all(me, peers, subs)
    for load in loads:
        load.start()
    nl = nl_ref[...]
    column = lax.broadcasted_iota(jnp.int32, (slots, halo), 1)
    repeat = jnp.where(
        lax.rem(column, slots) == lax.broadcasted_iota(jnp.int32, (slots, halo), 0), 1.0, 0.0
    )
    tiled = lax.dot_general(
        send_ref[0].astype(F32),
        repeat,
        (((0,), (0,)), ((), ())),
        precision=lax.Precision.HIGHEST,
        preferred_element_type=F32,
    )
    column = lax.broadcasted_iota(jnp.int32, (peers, halo), 1)
    peer = lax.broadcasted_iota(jnp.int32, (peers, halo), 0) * slots
    live = (column >= peer) & (column < peer + slots)
    slot_row = jnp.round(jnp.sum(jnp.where(live, tiled, 0.0), axis=0, keepdims=True))
    slot_col = jnp.transpose(jnp.broadcast_to(slot_row, (8, halo)))[:, 0:1]
    node_iota = lax.broadcasted_iota(jnp.int32, (halo, nodes), 1).astype(F32)
    picked = mm(one_hot(node_iota == slot_col), nl)
    halo_sent[...] = fold(picked.reshape(peers, slots, latent), 2).astype(BF16)
    pl.semaphore_wait(barrier, peers - 1)

    def halo_copy(d, target, slot):
        return pltpu.make_async_remote_copy(
            src_ref=halo_sent.at[target],
            dst_ref=halo_got.at[slot],
            send_sem=halo_send.at[d],
            recv_sem=halo_recv.at[d],
            device_id=place(target, subs),
            device_id_type=MESH,
        )

    @pl.loop(1, peers)
    def _(d):
        halo_copy(d, lax.rem(me + d, peers), me).start()

    halo_got[me] = halo_sent[me]
    table[pl.ds(0, nodes), :] = nl
    agg[...] = jnp.zeros_like(agg)
    sums[...] = jnp.zeros_like(sums)
    vec[...] = jnp.zeros_like(vec)
    rows[...] = jnp.concatenate(
        [
            jnp.broadcast_to(er_idx[...][None, :], (4, edges)),
            jnp.broadcast_to(es_idx[...][None, :] + nodes, (4, edges)),
        ],
        axis=0,
    ).astype(F32)
    cols[...] = jnp.transpose(rows[...])
    loads[0].wait()
    projected[pl.ds(0, nodes), :] = mm(nl, receiver[...]).astype(BF16)
    loads[1].wait()

    @pl.loop(0, steps)
    def _(t):
        at = pl.ds(pl.multiple_of(t * tile, tile), tile)
        iota = lax.broadcasted_iota(jnp.int32, (tile, total), 1).astype(F32)
        hot[at, :] = one_hot((cols[at, 0:1] == iota) | (cols[at, 4:5] == iota))
        iota_t = lax.broadcasted_iota(jnp.int32, (total, tile), 0).astype(F32)
        hot_t[:, at] = one_hot((rows[0:1, at] == iota_t) | (rows[4:5, at] == iota_t))
        dsilu_s[at, :] = mm(el_ref[at, :], first[...]) + eb_ref[...]

    @pl.loop(1, peers)
    def _(d):
        halo_copy(d, lax.rem(me + d, peers), lax.rem(me + peers - d, peers)).wait_recv()

    table[pl.ds(nodes, halo), :] = (
        unfold(halo_got[...].astype(F32), 2).reshape(halo, latent).astype(BF16)
    )
    projected[pl.ds(nodes, nodes + halo), :] = mm(table[...], sender[...]).astype(BF16)

    loads[2].wait()

    @pl.loop(0, steps)
    def _(t):
        at = pl.ds(pl.multiple_of(t * tile, tile), tile)
        active, dsilu = activate(dsilu_s[at, :] + mm(hot[at, :], projected[...]))
        active_s[at, :] = active
        dsilu_s[at, :] = dsilu
        normed, inverse = layer_norm(mm(active, es_ref[...]))
        normed_s[at, :] = normed
        inverse_s[at, :] = inverse
        message = (normed * eg_ref[...] + esh_ref[...]).astype(BF16)
        agg[...] += mm(hot_t[pl.ds(0, nodes), at], message)

    def own(c, q, s):
        g, col, width = chunks[c]
        m = shares[g]
        row = pl.multiple_of((q * subs + s) * m, 8)
        return fold(grads[g][pl.ds(row, m), pl.ds(col, width)], k)

    def near(c, stage, src, dst, target):
        return pltpu.make_async_remote_copy(
            src_ref=src,
            dst_ref=dst,
            send_sem=near_send.at[c, stage],
            recv_sem=near_recv.at[c, stage],
            device_id=target,
            device_id_type=MESH,
        )

    def of(c):
        return bufs[6 * c : 6 * c + 6]

    def copy_1(c):
        return near(c, 0, of(c)[0], of(c)[1], {"region": region, "sub": 1 - sub})

    def copy_2(c):
        other = region + 1 - 2 * inner
        return near(c, 1, of(c)[2], of(c)[3], {"region": other, "sub": sub})

    def copy_3(c, d, target, slot):
        return pltpu.make_async_remote_copy(
            src_ref=of(c)[4].at[target],
            dst_ref=of(c)[5].at[slot],
            send_sem=far_send.at[c, d],
            recv_sem=far_recv.at[c, d],
            device_id={"region": target * 2 + inner, "sub": sub},
            device_id_type=MESH,
        )

    def ret_copy(d, target, slot):
        return pltpu.make_async_remote_copy(
            src_ref=ret_ref.at[target],
            dst_ref=got.at[slot],
            send_sem=ret_send.at[d],
            recv_sem=ret_recv.at[d],
            device_id=place(target, subs),
            device_id_type=MESH,
        )

    def stage_1(c):
        a1 = of(c)[0]

        @pl.loop(0, regions)
        def _(q):
            a1[q] = own(c, q, 1 - sub).astype(BF16)

        copy_1(c).start()

    def stage_2(c):
        b1, a2 = of(c)[1:3]
        copy_1(c).wait_recv()

        @pl.loop(0, outer)
        def _(o):
            q = o * 2 + 1 - inner
            a2[o] = (own(c, q, sub) + b1[q].astype(F32)).astype(BF16)

        copy_2(c).start()

    def stage_3(c):
        b1, b2, a3 = of(c)[1], of(c)[3], of(c)[4]
        copy_2(c).wait_recv()

        @pl.loop(0, outer)
        def _(o):
            q = o * 2 + inner
            a3[o] = (own(c, q, sub) + b1[q].astype(F32) + b2[o].astype(F32)).astype(BF16)

        @pl.loop(1, outer)
        def _(d):
            copy_3(c, d, lax.rem(place_o + d, outer), place_o).start()

    def finish(c):
        b1, b2, b3 = of(c)[1], of(c)[3], of(c)[5]

        @pl.loop(1, outer)
        def _(d):
            source = lax.rem(place_o + outer - d, outer)
            copy_3(c, d, lax.rem(place_o + d, outer), source).wait_recv()

        result = own(c, region, sub) + b1[region].astype(F32) + b2[place_o].astype(F32)

        def add(d, value):
            return value + b3[lax.rem(place_o + d, outer)].astype(F32)

        g, col, width = chunks[c]
        value = unfold(lax.fori_loop(1, outer, add, result), k)
        small_out[pl.ds(starts[g], shares[g]), pl.ds(col, width)] = value

    node_chunks = [c for c, (g, _, _) in enumerate(chunks) if g < 2]
    second_chunks = [c for c, (g, _, _) in enumerate(chunks) if g == 2]
    first_chunks = [c for c, (g, _, _) in enumerate(chunks) if g == 3]

    loads[3].wait()
    loads[4].wait()
    aggregate = agg[...].astype(BF16)
    top = nf_ref.at[pl.ds(0, latent)]
    low = nf_ref.at[pl.ds(latent, latent)]
    before = mm(nl, top[...]) + mm(aggregate, low[...]) + nb_ref[...]
    active, dsilu = activate(before)
    normed, inverse = layer_norm(mm(active, ns_ref[...]))
    cot = nc_ref[...].astype(F32)
    grad_out = norm_backward(cot, ng_ref[...], normed, inverse)
    grad_before = mm_nt(grad_out, ns_ref[...]) * dsilu
    grad_pre = grad_before.astype(BF16)
    gns_ref[...] = mm_tn(active, grad_out) * node_scale
    gnf_ref[pl.ds(0, latent), :] = mm_tn(nl, grad_pre) * node_scale
    gnf_ref[pl.ds(latent, latent), :] = mm_tn(aggregate, grad_pre) * node_scale
    for c in node_chunks:
        stage_1(c)
    node_part[...] = cot + mm_nt(grad_pre, top[...])
    projected[pl.ds(0, nodes), :] = mm_nt(grad_pre, low[...]).astype(BF16)
    vec[3:4, :] = jnp.sum(grad_before, axis=0, keepdims=True) * node_scale
    vec[4:5, :] = jnp.sum(cot * normed, axis=0, keepdims=True) * node_scale
    gef_ref[pl.ds(0, latent), :] = jnp.zeros((latent, latent), F32)
    ges_ref[...] = jnp.zeros_like(ges_ref)

    loads[5].wait()

    @pl.loop(0, steps)
    def _(t):
        at = pl.ds(pl.multiple_of(t * tile, tile), tile)
        cot = ec_ref[at, :].astype(F32)
        grad = cot + mm(hot[at, pl.ds(0, nodes)], projected[pl.ds(0, nodes), :])
        normed = normed_s[at, :]
        grad_out = norm_backward(grad, eg_ref[...], normed, inverse_s[at, :])
        grad_out_s[at, :] = grad_out
        vec[1:2, :] += jnp.sum(grad * normed, axis=0, keepdims=True) * edge_scale
        vec[2:3, :] += jnp.sum(grad, axis=0, keepdims=True) * edge_scale
        ges_ref[...] += mm_tn(active_s[at, :], grad_out) * edge_scale

    for c in second_chunks:
        stage_1(c)
    for c in node_chunks:
        stage_2(c)

    @pl.loop(0, steps)
    def _(t):
        at = pl.ds(pl.multiple_of(t * tile, tile), tile)
        grad_before = mm_nt(grad_out_s[at, :], es_ref[...]) * dsilu_s[at, :]
        grad_pre = grad_before.astype(BF16)
        grad_pre_s[at, :] = grad_pre
        vec[0:1, :] += jnp.sum(grad_before, axis=0, keepdims=True) * edge_scale
        sums[...] += mm(hot_t[:, at], grad_pre)
        gef_ref[pl.ds(0, latent), :] += mm_tn(el_ref[at, :], grad_pre) * edge_scale

        @pl.when(t == min(1, steps - 1))
        def _():
            for c in second_chunks:
                stage_2(c)
            for c in node_chunks:
                stage_3(c)

    received = sums[pl.ds(0, nodes), :].astype(BF16)
    sent = sums[pl.ds(nodes, nodes + halo), :].astype(BF16)
    gef_ref[pl.ds(latent, latent), :] = mm_tn(table[...], sent) * edge_scale
    gef_ref[pl.ds(2 * latent, latent), :] = mm_tn(nl, received) * edge_scale
    for c in first_chunks:
        stage_1(c)
    back = mm_nt(sent, sender[...])
    ret_ref[...] = jnp.concatenate(
        [
            back[nodes:].reshape(peers, slots, latent),
            jnp.broadcast_to(vec[...][None], (peers, 8, latent)),
        ],
        axis=1,
    ).astype(BF16)
    for c in first_chunks:
        stage_2(c)

    @pl.loop(1, peers)
    def _(d):
        ret_copy(d, lax.rem(me + d, peers), me).start()

    got[me] = ret_ref[me]
    for c in second_chunks:
        stage_3(c)
    node_part[...] += back[:nodes] + mm_nt(received, receiver[...])

    def edge_copy(t):
        at = pl.ds(pl.multiple_of(t * tile, tile), tile)
        return pltpu.make_async_copy(edge_out.at[at], edge_hbm.at[at], out_sem.at[t])

    @pl.loop(0, steps)
    def _(t):
        at = pl.ds(pl.multiple_of(t * tile, tile), tile)
        cot = ec_ref[at, :].astype(F32)
        edge_out[at, :] = (cot + mm_nt(grad_pre_s[at, :], first[...])).astype(BF16)
        edge_copy(t).start()

    for c in first_chunks:
        stage_3(c)
    for c in node_chunks + second_chunks:
        finish(c)

    @pl.loop(1, peers)
    def _(d):
        ret_copy(d, lax.rem(me + d, peers), lax.rem(me + peers - d, peers)).wait_recv()

    arrived = got[...].astype(F32)
    vectors = jnp.sum(arrived[:, slots:], axis=0)
    width = latent // peers
    mine = jnp.zeros((8, width), F32)
    for p in range(peers):
        mine = jnp.where(me == p, vectors[:, p * width : (p + 1) * width], mine)
    small_out[pl.ds(starts[4], 8), pl.ds(0, width)] = mine
    returned = arrived[:, :slots].reshape(halo, latent).astype(BF16)
    spread = one_hot(
        lax.broadcasted_iota(jnp.int32, (nodes, halo), 0).astype(F32) == slot_row
    )
    small_out[pl.ds(starts[4] + 8, nodes), :] = node_part[...] + mm(spread, returned)
    for c in first_chunks:
        finish(c)

    @pl.loop(0, steps)
    def _(t):
        edge_copy(t).wait()

    for c in range(len(chunks)):
        copy_1(c).wait_send()
        copy_2(c).wait_send()

        @pl.loop(1, outer)
        def _(d, c=c):
            copy_3(c, d, lax.rem(place_o + d, outer), place_o).wait_send()

    @pl.loop(1, peers)
    def _(d):
        halo_copy(d, lax.rem(me + d, peers), me).wait_send()
        ret_copy(d, lax.rem(me + d, peers), me).wait_send()


def split_kernel(
    small_ref,
    edge_ref,
    node_out,
    gns_out,
    gnf_out,
    ges_out,
    gef_out,
    ev_out,
    nv_out,
    edge_out,
    held,
    in_sem,
    out_sem,
):
    parts = in_sem.shape[0]
    each = edge_ref.shape[0] // parts
    pieces = [pl.ds(j * each, each) for j in range(parts)]
    loads = [
        pltpu.make_async_copy(edge_ref.at[at], held.at[at], in_sem.at[j])
        for j, at in enumerate(pieces)
    ]
    stores = [
        pltpu.make_async_copy(held.at[at], edge_out.at[at], out_sem.at[j])
        for j, at in enumerate(pieces)
    ]
    for load in loads:
        load.start()
    for load, store in zip(loads, stores):
        load.wait()
        store.start()
    row = 0
    for out in (gns_out, gnf_out, ges_out, gef_out):
        out[...] = small_ref[pl.ds(row, out.shape[0]), :]
        row += out.shape[0]
    width = ev_out.shape[1]
    vectors = small_ref[pl.ds(row, 8), :]
    ev_out[...] = vectors[0:3, :width]
    nv_out[...] = vectors[3:5, :width]
    node_out[...] = small_ref[pl.ds(row + 8, node_out.shape[0]), :].astype(BF16)
    for store in stores:
        store.wait()


def in_vmem(count):
    return [pl.BlockSpec(memory_space=pltpu.VMEM)] * count


def on_device(
    regions,
    subs,
    node_latent,
    edge_latent,
    node_cot,
    edge_cot,
    send_rows,
    edge_sender,
    edge_receiver,
    edge_first,
    edge_second,
    edge_bias,
    edge_gain,
    edge_shift,
    node_first,
    node_second,
    node_bias,
    node_gain,
):
    peers = regions * subs
    nodes, latent = node_latent.shape
    edges = edge_latent.shape[0]
    slots = send_rows.shape[2]
    halo = peers * slots
    total = 2 * nodes + halo
    shape = jax.ShapeDtypeStruct
    tile = math.gcd(edges, 512)
    row = lambda x: x.reshape(1, -1)

    weights = (node_second, node_first, edge_second, edge_first)
    shares = [w.shape[0] // peers for w in weights]
    k = 1 if all(m % 16 == 0 for m in shares) else 2
    half = latent // 2
    chunks = ((0, 0, latent), (1, 0, half), (1, half, half))
    chunks += ((2, 0, latent), (3, 0, half), (3, half, half))
    outer = regions // 2
    sem = pltpu.SemaphoreType.DMA
    count = len(chunks)
    scratch = [
        pltpu.VMEM((edges, latent), BF16),
        pltpu.VMEM((edges, latent), BF16),
        pltpu.VMEM(edge_first.shape, BF16),
        pltpu.VMEM(edge_second.shape, BF16),
        pltpu.VMEM(node_first.shape, BF16),
        pltpu.VMEM(node_second.shape, BF16),
        pltpu.VMEM((edges, latent), BF16),
        pltpu.VMEM((edges, latent), BF16),
        pltpu.VMEM((edges, latent), BF16),
        sem((6,)),
        sem((edges // tile,)),
        pltpu.VMEM((edges, total), BF16),
        pltpu.VMEM((total, edges), BF16),
        pltpu.VMEM((8, edges), F32),
        pltpu.VMEM((edges, 8), F32),
        pltpu.VMEM((nodes + halo, latent), BF16),
        pltpu.VMEM((total, latent), BF16),
        pltpu.VMEM((edges, latent), BF16),
        pltpu.VMEM((edges, latent), F32),
        pltpu.VMEM((edges, latent), F32),
        pltpu.VMEM((edges, 1), F32),
        pltpu.VMEM((nodes, latent), F32),
        pltpu.VMEM((total, latent), F32),
        pltpu.VMEM((8, latent), F32),
        pltpu.VMEM((nodes, latent), F32),
        *(pltpu.VMEM(w.shape, F32) for w in weights),
        pltpu.VMEM((peers, 2 * slots, half), BF16),
        pltpu.VMEM((peers, 2 * slots, half), BF16),
        pltpu.VMEM((peers, slots + 8, latent), BF16),
        pltpu.VMEM((peers, slots + 8, latent), BF16),
        sem((peers,)),
        sem((peers,)),
        sem((peers,)),
        sem((peers,)),
        sem((count, 2)),
        sem((count, 2)),
        sem((count, outer)),
        sem((count, outer)),
    ]
    for g, _, width in chunks:
        for lead in (regions, regions, outer, outer, outer, outer):
            scratch.append(pltpu.VMEM((lead, shares[g] * k, width // k), BF16))
    parts = math.gcd(edges // 16, 8)
    in_hbm = pl.BlockSpec(memory_space=pl.ANY)
    small_rows = sum(shares) + 8 + nodes
    edge_grad, small = pl.pallas_call(
        functools.partial(layer_kernel, regions, subs, tile, k, chunks),
        out_shape=(shape((edges, latent), BF16), shape((small_rows, latent), F32)),
        in_specs=[in_hbm if j in (1, 3, 7, 8, 12, 13) else in_vmem(1)[0] for j in range(16)],
        out_specs=(in_hbm, *in_vmem(1)),
        scratch_shapes=scratch,
        compiler_params=pltpu.CompilerParams(
            collective_id=0, has_side_effects=True, vmem_limit_bytes=VMEM_LIMIT
        ),
    )(
        node_latent,
        edge_latent,
        node_cot,
        edge_cot,
        jnp.swapaxes(send_rows, 1, 2),
        edge_sender,
        edge_receiver,
        edge_first,
        edge_second,
        row(edge_bias),
        row(edge_gain),
        row(edge_shift),
        node_first,
        node_second,
        row(node_bias),
        row(node_gain),
    )
    width = latent // peers
    node_grad, gns, gnf, ges, gef, ev, nv, edge_grad = pl.pallas_call(
        split_kernel,
        out_shape=(
            shape((nodes, latent), BF16),
            *(shape((m, latent), F32) for m in shares),
            shape((3, width), F32),
            shape((2, width), F32),
            shape((edges, latent), BF16),
        ),
        in_specs=[*in_vmem(1), in_hbm],
        out_specs=(*in_vmem(7), in_hbm),
        scratch_shapes=[pltpu.VMEM((edges, latent), BF16), sem((parts,)), sem((parts,))],
        compiler_params=pltpu.CompilerParams(vmem_limit_bytes=VMEM_LIMIT),
    )(small, edge_grad)
    return node_grad, edge_grad, gef, ges, ev, gnf, gns, nv


def solution(mesh):
    spread = P(("group", "region", "sub"), None)
    flat = P(("group", "region", "sub"))
    vector = P("group", ("region", "sub"))
    return jax.shard_map(
        functools.partial(on_device, mesh.shape["region"], mesh.shape["sub"]),
        mesh=mesh,
        in_specs=(
            spread,
            spread,
            spread,
            spread,
            P(("group", "region", "sub"), None, None),
            flat,
            flat,
        )
        + (P(),) * 9,
        out_specs=(spread, spread, spread, spread, vector, spread, spread, vector),
        check_vma=False,
    )
```
